256 devices in a mesh: inst: 16 (over y_lo, z), blk: 16 (over y_hi, x, core).
Axes of the slice: x: 4, y: 4 (y_hi: 2, y_lo: 2; y = y_hi * 2 + y_lo), z: 8, core: 2. Of those that a mesh axis runs over, the one named last changes fastest.
Arguments:
- state: float32 [16, 5, 32, 128, 128], P('inst', None, 'blk'), may hold values from -6 to 6
- row_jacobian: float32 [5, 5], replicated, may hold values from -2.5 to 2.5
- cell_jacobian: float32 [5, 5], replicated, may hold values from -2.5 to 2.5
- viscosity: float32 [32, 128, 128], P('blk'), may hold values from 0.05 to 1
- local_step: float32 [32, 128, 128], P('blk'), may hold values from 0.02 to 0.1
- live_rows: int32 [32], replicated, may hold values from 1 to 128, 3072 in all
- partner: int32 [64], replicated, may hold values from 0 to 63, as said below
Outputs:
- new_state: float32 [16, 5, 32, 128, 128], P('inst', None, 'blk')
- final_residual: float32 [16, 5, 32, 128, 128], P('inst', None, 'blk')
The draws below stay inside these ranges and needn't reach their ends.
Inputs may be any that keep to these rules, and one draw needn't show every extreme that they name: partner pairs the faces: partner[partner[f]] = f and partner[f] differs from f.
All inputs are finite; a program needn't handle non-finite values.
Results may differ from the reference program's by a relative error of at most 0.000058.
Values sent between devices are 32-bit elements; how exact they have to be, the bound alone decides.
No kernel may reach another device: no remote copies, remote signals or barrier semaphores. Data moves between devices by JAX's collectives and lax.ppermute only.
A program may use at most 64 MiB of HBM per device.

```python
import math
import jax
import jax.numpy as jnp
import numpy as np
from jax import lax

VARS = 5
CELLS = 128
ROWS = 128
INST = 16
BLOCKS = 32


def draw_partner(key, part):
    key = jax.random.fold_in(key, 7)
    order = jax.random.permutation(key, 2 * BLOCKS).astype(jnp.int32)
    pairs = order.reshape(BLOCKS, 2)
    result = jnp.zeros((2 * BLOCKS,), jnp.int32)
    result = result.at[pairs[:, 0]].set(pairs[:, 1])
    result = result.at[pairs[:, 1]].set(pairs[:, 0])
    return result.astype(jnp.int32)


def block_scale(rng, dims, shards, smallest, top_value):
    level, own = 1.0, jax.random.fold_in(rng, 6)
    for axis_at, shards_of in shards:
        steps = jnp.exp(jax.random.uniform(jax.random.fold_in(own, axis_at), (shards_of,), jnp.float32, smallest / len(shards), top_value / len(shards)))
        level = level * jnp.repeat(steps, dims[axis_at] // shards_of).reshape([-1 if axis == axis_at else 1 for axis in range(len(dims))])
    return level


def length_profile(amount, total, limit, slope):
    weights = [(1 << 20) // math.isqrt(standing ** slope) + 1 for standing in range(2, amount + 1)]
    spare, holding = total - limit - (amount - 1), [1] * (amount - 1)
    while spare > 0:
        free = [i for i in range(amount - 1) if holding[i] < limit]
        mass, left = sum([weights[i] for i in free]), spare
        for i in free:
            addition = min(limit - holding[i], max(1, left * weights[i] // mass), spare)
            holding[i] = holding[i] + addition
            spare = spare - addition
    return np.array([limit] + holding)


def ragged_sizes(stream_key, amount, total, limit, slope):
    if amount == 2:
        one = jax.random.randint(stream_key, (), max(1, total - limit), min(limit, total - 1) + 1)
        return jnp.stack([one, total - one])
    tallies = jnp.asarray(length_profile(amount, total, limit, slope), jnp.int32)
    twos = (amount - 1) // 2
    giver, sink = tallies[1:1 + 2 * twos:2], tallies[2:2 + 2 * twos:2]
    room = jnp.minimum(giver - 1, limit - sink)
    moved = jax.random.randint(jax.random.fold_in(stream_key, 1), (twos,), 0, 1 << 20) % (room + 1)
    tallies = tallies.at[1:1 + 2 * twos:2].set(giver - moved).at[2:2 + 2 * twos:2].set(sink + moved)
    return tallies[jax.random.permutation(jax.random.fold_in(stream_key, 2), amount)]


def bell_draw(own_key, dims, scale, limit, pieces=(), kind=jnp.bfloat16):
    drawn = scale * jax.random.normal(own_key, dims, jnp.float32)
    if pieces:
        drawn = drawn * block_scale(own_key, dims, pieces, -0.22, 0.18)
    return jnp.clip(drawn, -limit, limit).astype(kind)


def setup_inputs(seed: int = 0) -> dict:
    seeds = jax.random.split(jax.random.key(seed), 8)
    state = bell_draw(seeds[0], (INST, VARS, BLOCKS, ROWS, CELLS), 1.0, 6.0, ((0, 16), (2, 16)), jnp.float32)
    row_jacobian = bell_draw(seeds[1], (VARS, VARS), VARS ** -0.5, 2.5, (), jnp.float32)
    cell_jacobian = bell_draw(seeds[2], (VARS, VARS), VARS ** -0.5, 2.5, (), jnp.float32)
    viscosity = jnp.clip(jnp.exp(math.log(1.0) - 2.9957323 * jax.random.uniform(seeds[3], (BLOCKS, ROWS, CELLS), jnp.float32) ** block_scale(seeds[3], (BLOCKS, ROWS, CELLS), ((0, 16),), -0.2, 0.2)), 0.05, 1.0)
    local_step = jnp.clip(jnp.exp(math.log(0.1) - 1.609438 * jax.random.uniform(seeds[4], (BLOCKS, ROWS, CELLS), jnp.float32) ** block_scale(seeds[4], (BLOCKS, ROWS, CELLS), ((0, 16),), -0.2, 0.2)), 0.02, 0.1)
    live_rows = ragged_sizes(seeds[5], BLOCKS, BLOCKS * ROWS * 3 // 4, ROWS, 2).astype(jnp.int32)
    partner = draw_partner(jax.random.fold_in(seeds[7], 71), 0)
    return {"state": state, "row_jacobian": row_jacobian, "cell_jacobian": cell_jacobian, "viscosity": viscosity, "local_step": local_step, "live_rows": live_rows, "partner": partner}


precise = lax.Precision.HIGHEST


def spectral_matrix(count):
    numbers = jnp.arange(count, dtype=jnp.int32)
    offset = (numbers[:, None] - numbers[None, :]) % count
    angle = jnp.pi * offset.astype(jnp.float32) / count
    parity = 1.0 - 2.0 * (offset % 2).astype(jnp.float32)
    sine = jnp.where(offset == 0, 1.0, jnp.sin(angle))
    return jnp.where(offset == 0, 0.0, 0.5 * parity * jnp.cos(angle) / sine).astype(jnp.float32)


def evaluate(state, row_jacobian, cell_jacobian, viscosity, live_rows, partner):
    instances, variables, blocks, height, width = state.shape
    row_index = jnp.arange(height, dtype=jnp.int32)
    last_mask = (row_index[None, :] == (live_rows - 1)[:, None])[:, :, None]
    upper = jnp.sum(jnp.where(last_mask, state, 0.0), axis=3)
    lower = state[:, :, :, 0, :]
    face_rows = jnp.stack([lower, upper], axis=3).reshape(instances, variables, 2 * blocks, width)
    ghosts = face_rows[:, :, partner, :].reshape(instances, variables, blocks, 2, width)
    previous = jnp.concatenate([ghosts[:, :, :, 0:1, :], state[:, :, :, :-1, :]], axis=3)
    shifted = jnp.concatenate([state[:, :, :, 1:, :], jnp.zeros_like(state[:, :, :, :1, :])], axis=3)
    edge_mask = (row_index[None, :] + 1 == live_rows[:, None])[:, :, None]
    following = jnp.where(edge_mask, ghosts[:, :, :, 1:2, :], shifted)
    east = jnp.roll(state, -1, axis=4)
    west = jnp.roll(state, 1, axis=4)
    convect = 0.5 * jnp.einsum('uv,tvbrc->tubrc', row_jacobian, following - previous, precision=precise)
    convect = convect + 0.5 * jnp.einsum('uv,tvbrc->tubrc', cell_jacobian, east - west, precision=precise)
    damping = (0.25 + viscosity) * ((following - 2.0 * state + previous) + (east - 2.0 * state + west))
    spectral = jnp.einsum('ts,svbrc->tvbrc', spectral_matrix(instances), state, precision=precise)
    live_mask = (row_index[None, :] < live_rows[:, None])[:, :, None]
    return jnp.where(live_mask, spectral + convect - damping, 0.0)


def reference(state, row_jacobian, cell_jacobian, viscosity, local_step, live_rows, partner):
    first = evaluate(state, row_jacobian, cell_jacobian, viscosity, live_rows, partner)
    half_state = state - 0.5 * local_step * first
    final_residual = evaluate(half_state, row_jacobian, cell_jacobian, viscosity, live_rows, partner)
    return state - local_step * final_residual, final_residual
```

```python
import functools
import math

import jax
import jax.numpy as jnp
from jax import lax
from jax.experimental import pallas as pl
from jax.experimental.pallas import tpu as pltpu
from jax.sharding import PartitionSpec as P

VARS, BLOCKS, ROWS, CELLS, INST = 5, 2, 128, 128, 16
SLAB = 16
PER_BLOCK = ROWS // SLAB
MAIN = VARS * SLAB
PREV, NEXT, FACE = MAIN, MAIN + VARS, MAIN + 2 * VARS
SENT = 112
FACES = 2 * BLOCKS
VMEM = pl.BlockSpec(memory_space=pltpu.VMEM)
SMEM = pl.BlockSpec(memory_space=pltpu.SMEM)
PARAMS = pltpu.CompilerParams(vmem_limit_bytes=32 * 1024 * 1024)


def spectral(m):
    m = m % INST
    if m in (0, INST // 2):
        return 0.0
    return 0.5 * (-1.0) ** m * math.cos(math.pi * m / INST) / math.sin(math.pi * m / INST)


HALF = INST // 2
EVEN = [0.5 * (spectral(m) + spectral(m + HALF)) for m in range(HALF)]
ODD = [0.5 * (spectral(m) - spectral(m + HALF)) for m in range(HALF)]


def weighted(terms):
    total = None
    for weight, value in terms:
        term = weight * value
        total = term if total is None else total + term
    return total


def apply_even(p):
    return [
        weighted([(EVEN[m], p[(t - m) % HALF] - p[(t + m) % HALF]) for m in range(1, HALF // 2)])
        for t in range(HALF)
    ]


def apply_odd(q):
    def at(index):
        index %= INST
        return q[index] if index < HALF else -q[index - HALF]

    def pair(t, m):
        low, high = (t - m) % INST, (t + m) % INST
        first = q[low % HALF] if low < HALF else None
        second = q[high % HALF] if high < HALF else None
        a, b = q[low % HALF], q[high % HALF]
        if first is not None and second is not None:
            return a - b, 1.0
        if first is None and second is not None:
            return a + b, -1.0
        if first is not None:
            return a + b, 1.0
        return a - b, -1.0

    result = []
    for t in range(HALF):
        terms = []
        for m in range(1, HALF // 2):
            value, sign = pair(t, m)
            terms.append((sign * ODD[m], value))
        last = (t - HALF // 2) % INST
        terms.append((ODD[HALF // 2] if last < HALF else -ODD[HALF // 2], q[last % HALF]))
        result.append(weighted(terms))
    return result


def row_shifts(tile, before, after):
    rows = tile.shape[0]
    row = lax.broadcasted_iota(jnp.int32, tile.shape, 0)
    following = jnp.where(row == rows - 1, after, pltpu.roll(tile, rows - 1, 0))
    previous = jnp.where(row == 0, before, pltpu.roll(tile, 1, 0))
    return following, previous


def east_west(tile):
    return pltpu.roll(tile, CELLS - 1, 1), pltpu.roll(tile, 1, 1)


def pack_kernel(live_ref, state_ref, chunks_ref, faces_ref):
    first = lax.axis_index("blk") * BLOCKS
    for b in range(BLOCKS):
        last = live_ref[first + b] - 1
        for v in range(VARS):
            faces_ref[pl.ds((2 * b) * VARS + v, 1), :] = state_ref[0, v, b, 0:1, :]
            faces_ref[pl.ds((2 * b + 1) * VARS + v, 1), :] = state_ref[0, v, b, pl.ds(last, 1), :]
    faces = faces_ref[...]
    for b in range(BLOCKS):
        for j in range(PER_BLOCK):
            i = b * PER_BLOCK + j
            low = j * SLAB
            for v in range(VARS):
                chunks_ref[i, v * SLAB : (v + 1) * SLAB, :] = state_ref[0, v, b, low : low + SLAB, :]
                before, after = max(low - 1, 0), min(low + SLAB, ROWS - 1)
                chunks_ref[i, PREV + v : PREV + v + 1, :] = state_ref[0, v, b, before : before + 1, :]
                chunks_ref[i, NEXT + v : NEXT + v + 1, :] = state_ref[0, v, b, after : after + 1, :]
            chunks_ref[i, FACE : FACE + FACES * VARS, :] = faces
            chunks_ref[i, FACE + FACES * VARS : SENT, :] = jnp.zeros((SENT - FACE - FACES * VARS, CELLS), jnp.float32)


def ghost_place(partner_ref, face):
    me = lax.axis_index("blk")
    other = partner_ref[me * FACES + face]
    device, local = other // FACES, other % FACES
    core = (device % 2 + me % 2) % 2
    x = ((device // 2) % 4 - (me // 2) % 4 + 4) % 4
    y = (device // 8 + me // 8) % 2
    return (core * 4 + x) * 2 + y, local


def spatial_kernel(live_ref, partner_ref, row_ref, cell_ref, state_ref, visc_ref, step_ref, gathered_ref,
                   spatial_ref, faces_ref, half_ref):
    first = lax.axis_index("blk") * BLOCKS

    def stencil(tiles, befores, afters, mask_n, mask_p, damp):
        across, along, smooth = [], [], []
        for v in range(VARS):
            n, p = row_shifts(tiles[v], befores[v], afters[v])
            n, p = n * mask_n, p * mask_p
            e, w = east_west(tiles[v])
            across.append(n - p)
            along.append(e - w)
            smooth.append((n + p) + (e + w) - 4.0 * tiles[v])
        result = []
        for u in range(VARS):
            total = -damp * smooth[u]
            for v in range(VARS):
                total = total + (0.5 * row_ref[u, v]) * across[v] + (0.5 * cell_ref[u, v]) * along[v]
            result.append(total)
        return result

    def sweep(read, write, b, live):
        def step(j, carry):
            low = pl.multiple_of(j * SLAB, SLAB)
            before, after = jnp.maximum(low - 1, 0), jnp.minimum(low + SLAB, ROWS - 1)
            row = low + lax.broadcasted_iota(jnp.int32, (SLAB, CELLS), 0)
            mask_n = jnp.where(row + 1 < live, 1.0, 0.0)
            mask_p = jnp.where(row > 0, 1.0, 0.0)
            damp = 0.25 + visc_ref[b, pl.ds(low, SLAB), :]
            tiles = [read(v, b, pl.ds(low, SLAB)) for v in range(VARS)]
            befores = [read(v, b, pl.ds(before, 1)) for v in range(VARS)]
            afters = [read(v, b, pl.ds(after, 1)) for v in range(VARS)]
            result = stencil(tiles, befores, afters, mask_n, mask_p, damp)
            write(b, low, tiles, result)
            return carry

        lax.fori_loop(0, PER_BLOCK, step, 0)

    def read_state(v, b, rows):
        return state_ref[0, v, b, rows, :]

    def read_half(v, b, rows):
        return half_ref[v, b, rows, :]

    def write_half(b, low, tiles, result):
        scale = 0.5 * step_ref[b, pl.ds(low, SLAB), :]
        for v in range(VARS):
            half_ref[v, b, pl.ds(low, SLAB), :] = tiles[v] - scale * result[v]

    def write_spatial(b, low, tiles, result):
        for v in range(VARS):
            spatial_ref[v, b, pl.ds(low, SLAB), :] = result[v]

    for b in range(BLOCKS):
        live = live_ref[first + b]
        sweep(read_state, write_half, b, live)
        for side in range(2):
            place, local = ghost_place(partner_ref, 2 * b + side)
            row = (live - 1) if side else 0
            sign = 0.5 if side else -0.5
            rows = pl.ds(row, 1)
            ghost = [gathered_ref[place, pl.ds(local * VARS + v, 1), :] for v in range(VARS)]
            damp = 0.25 + visc_ref[b, rows, :]
            scale = 0.5 * step_ref[b, rows, :]
            for u in range(VARS):
                total = -damp * ghost[u]
                for v in range(VARS):
                    total = total + (sign * row_ref[u, v]) * ghost[v]
                half_ref[u, b, rows, :] = half_ref[u, b, rows, :] - scale * total
        for side in range(2):
            row = (live - 1) if side else 0
            for v in range(VARS):
                faces_ref[pl.ds((2 * b + side) * VARS + v, 1), :] = half_ref[v, b, pl.ds(row, 1), :]
        sweep(read_half, write_spatial, b, live)


def slab_kernel(live_ref, row_ref, cell_ref, got_ref, visc_ref, step_ref, sent_ref, rate_ref):
    i = lax.axis_index("inst")
    b, j = i // PER_BLOCK, i % PER_BLOCK
    live = live_ref[lax.axis_index("blk") * BLOCKS + b]
    low = pl.multiple_of(j * SLAB, SLAB)
    step = step_ref[b, pl.ds(low, SLAB), :]
    step_before = step_ref[b, pl.ds(jnp.maximum(low - 1, 0), 1), :]
    step_after = step_ref[b, pl.ds(jnp.minimum(low + SLAB, ROWS - 1), 1), :]
    row = low + lax.broadcasted_iota(jnp.int32, (SLAB, CELLS), 0)
    step_n, step_p = row_shifts(step, step_before, step_after)
    step_e, step_w = east_west(step)
    scale_n = jnp.where(row + 1 < live, step + step_n, 0.0)
    scale_p = jnp.where(row > 0, step + step_p, 0.0)
    scale_e, scale_w = step + step_e, step + step_w
    damp = 0.5 * (0.25 + visc_ref[b, pl.ds(low, SLAB), :])
    centre = 8.0 * step

    def times(rows, with_second):
        values = [got_ref[t, rows, :] for t in range(INST)]
        p = [values[t] + values[t + HALF] for t in range(HALF)]
        q = [values[t] - values[t + HALF] for t in range(HALF)]
        p, q = apply_even(p), apply_odd(q)
        for t in range(HALF):
            rate_ref[t, rows, :] = p[t] + q[t]
            rate_ref[t + HALF, rows, :] = p[t] - q[t]
        if with_second is not None:
            p, q = apply_even(p), apply_odd(q)
            for t in range(HALF):
                sent_ref[t, rows, :] = with_second * (p[t] + q[t])
                sent_ref[t + HALF, rows, :] = with_second * (p[t] - q[t])

    half_step = [-step[0:8, :], -step[8:16, :]]
    for v in range(VARS):
        for k in range(2):
            at = v * SLAB + 8 * k
            times(slice(at, at + 8), half_step[k])
    times(slice(MAIN, MAIN + 8), None)
    times(slice(MAIN + 8, MAIN + 16), None)

    def instance(t, carry):
        across, along, smooth, rates = [], [], [], []
        for v in range(VARS):
            rate = rate_ref[t, pl.ds(v * SLAB, SLAB), :]
            n, p = row_shifts(rate, rate_ref[t, PREV + v : PREV + v + 1, :], rate_ref[t, NEXT + v : NEXT + v + 1, :])
            e, w = east_west(rate)
            n, p, e, w = scale_n * n, scale_p * p, scale_e * e, scale_w * w
            across.append(n - p)
            along.append(e - w)
            smooth.append((n + p) + (e + w) - centre * rate)
            rates.append(rate)
        for u in range(VARS):
            rows = pl.ds(u * SLAB, SLAB)
            total = sent_ref[t, rows, :] + rates[u] + damp * smooth[u]
            for v in range(VARS):
                total = total - (0.25 * row_ref[u, v]) * across[v] - (0.25 * cell_ref[u, v]) * along[v]
            sent_ref[t, rows, :] = total
        return carry

    lax.fori_loop(0, INST, instance, 0)


def face_kernel(live_ref, weights_ref, got_ref, half_ref, step_ref, out_ref):
    first = lax.axis_index("blk") * BLOCKS
    me = lax.axis_index("inst")
    total = jnp.zeros((FACES * VARS, CELLS), jnp.float32)
    for s in range(INST):
        total = total + weights_ref[me, s] * got_ref[s, FACE : FACE + FACES * VARS, :]
    out_ref[FACES * VARS :, :] = total
    for b in range(BLOCKS):
        for side in range(2):
            row = (live_ref[first + b] - 1) if side else 0
            scale = 0.5 * step_ref[b, pl.ds(row, 1), :]
            at = (2 * b + side) * VARS
            out_ref[at : at + VARS, :] = half_ref[at : at + VARS, :] - scale * total[at : at + VARS, :]


def final_kernel(live_ref, partner_ref, row_ref, state_ref, visc_ref, step_ref, spatial_ref, got_ref, gathered_ref,
                 new_ref, residual_ref):
    first = lax.axis_index("blk") * BLOCKS
    for b in range(BLOCKS):
        live = live_ref[first + b]
        for j in range(PER_BLOCK):
            low = j * SLAB
            rows = slice(low, low + SLAB)
            row = low + lax.broadcasted_iota(jnp.int32, (SLAB, CELLS), 0)
            step = step_ref[b, rows, :]
            for v in range(VARS):
                total = got_ref[b * PER_BLOCK + j, v * SLAB : (v + 1) * SLAB, :] + spatial_ref[v, b, rows, :]
                total = jnp.where(row < live, total, 0.0)
                residual_ref[0, v, b, rows, :] = total
                new_ref[0, v, b, rows, :] = state_ref[0, v, b, rows, :] - step * total
        for side in range(2):
            place, local = ghost_place(partner_ref, 2 * b + side)
            row = (live - 1) if side else 0
            sign = 0.5 if side else -0.5
            rows = pl.ds(row, 1)
            step = step_ref[b, rows, :]
            damp = 0.25 + visc_ref[b, rows, :]
            ghost = [
                gathered_ref[place, pl.ds(local * VARS + v, 1), :]
                - 0.5 * step * gathered_ref[place, pl.ds((FACES + local) * VARS + v, 1), :]
                for v in range(VARS)
            ]
            for u in range(VARS):
                total = -damp * ghost[u]
                for v in range(VARS):
                    total = total + (sign * row_ref[u, v]) * ghost[v]
                residual_ref[0, u, b, rows, :] = residual_ref[0, u, b, rows, :] + total
                new_ref[0, u, b, rows, :] = new_ref[0, u, b, rows, :] - step * total


def call(body, outs, in_specs, scratch=(), name=None):
    return pl.pallas_call(
        body,
        out_shape=[jax.ShapeDtypeStruct(shape, jnp.float32) for shape in outs],
        in_specs=in_specs,
        out_specs=[VMEM] * len(outs),
        scratch_shapes=[pltpu.VMEM(shape, jnp.float32) for shape in scratch],
        compiler_params=PARAMS,
        name=name,
    )


def gathered_over_blocks(value):
    def moved(array, y, x, core):
        pairs = []
        for to in range(16):
            source = ((to // 8 + y) % 2) * 8 + (((to // 2) % 4 + x) % 4) * 2 + (to + core) % 2
            pairs.append((source, to))
        return lax.ppermute(array, "blk", pairs)

    value = value[None]
    value = jnp.concatenate([value, moved(value, 1, 0, 0)])
    value = jnp.concatenate([value] + [moved(value, 0, x, 0) for x in (1, 2, 3)])
    return jnp.concatenate([value, moved(value, 0, 0, 1)])


def per_device(state, row_jacobian, cell_jacobian, viscosity, local_step, live_rows, partner):
    whole = state.shape
    chunks, faces = call(
        pack_kernel, [(INST, SENT, CELLS), (FACES * VARS, CELLS)], [SMEM, VMEM], name="pack"
    )(live_rows, state)
    slabs = lax.all_to_all(chunks, "inst", 0, 0, tiled=True)
    ghosts = gathered_over_blocks(faces)
    spatial, half_faces = call(
        spatial_kernel,
        [(VARS, BLOCKS, ROWS, CELLS), (FACES * VARS, CELLS)],
        [SMEM, SMEM, SMEM, SMEM, VMEM, VMEM, VMEM, VMEM],
        [(VARS, BLOCKS, ROWS, CELLS)],
        name="spatial",
    )(live_rows, partner, row_jacobian, cell_jacobian, state, viscosity, local_step, ghosts)
    slabs, spatial = lax.optimization_barrier((slabs, spatial))
    (sent,) = call(
        slab_kernel, [(INST, MAIN, CELLS)], [SMEM, SMEM, SMEM, VMEM, VMEM, VMEM], [(INST, 96, CELLS)], name="slab"
    )(live_rows, row_jacobian, cell_jacobian, slabs, viscosity, local_step)
    back = lax.all_to_all(sent, "inst", 0, 0, tiled=True)
    weights = jnp.array([[spectral(t - s) for s in range(INST)] for t in range(INST)], jnp.float32)
    (faces2,) = call(
        face_kernel, [(2 * FACES * VARS, CELLS)], [SMEM, SMEM, VMEM, VMEM, VMEM], name="faces"
    )(live_rows, weights, slabs, half_faces, local_step)
    ghosts2 = gathered_over_blocks(faces2)
    new_state, residual = call(
        final_kernel, [whole, whole], [SMEM, SMEM, SMEM] + [VMEM] * 6, name="final"
    )(live_rows, partner, row_jacobian, state, viscosity, local_step, spatial, back, ghosts2)
    return new_state, residual


def solution(mesh):
    return jax.shard_map(
        per_device,
        mesh=mesh,
        in_specs=(
            P("inst", None, "blk", None, None),
            P(),
            P(),
            P("blk", None, None),
            P("blk", None, None),
            P(),
            P(),
        ),
        out_specs=(P("inst", None, "blk", None, None), P("inst", None, "blk", None, None)),
        check_vma=False,
    )
```

```python
import functools
import math

import jax
import jax.numpy as jnp
from jax import lax
from jax.experimental import pallas as pl
from jax.experimental.pallas import tpu as pltpu
from jax.sharding import PartitionSpec as P

VARS, BLOCKS, ROWS, CELLS, INST = 5, 2, 128, 128, 16
SLAB = 16
PER_BLOCK = ROWS // SLAB
MAIN = VARS * SLAB
PREV, NEXT, FACE = MAIN, MAIN + VARS, MAIN + 2 * VARS
SENT = 112
FACES = 2 * BLOCKS
VMEM = pl.BlockSpec(memory_space=pltpu.VMEM)
SMEM = pl.BlockSpec(memory_space=pltpu.SMEM)
HBM = pl.BlockSpec(memory_space=pltpu.HBM)

LIVE = pltpu.SMEM((32,), jnp.int32)
PARTNER = pltpu.SMEM((64,), jnp.int32)
JACOBIAN = pltpu.SMEM((VARS, VARS), jnp.float32)


def spectral(m):
    m = m % INST
    if m in (0, INST // 2):
        return 0.0
    return 0.5 * (-1.0) ** m * math.cos(math.pi * m / INST) / math.sin(math.pi * m / INST)


HALF = INST // 2
EVEN = [0.5 * (spectral(m) + spectral(m + HALF)) for m in range(HALF)]
ODD = [0.5 * (spectral(m) - spectral(m + HALF)) for m in range(HALF)]


def weighted(terms):
    total = None
    for weight, value in terms:
        term = weight * value
        total = term if total is None else total + term
    return total


def apply_even(p):
    return [
        weighted([(EVEN[m], p[(t - m) % HALF] - p[(t + m) % HALF]) for m in range(1, HALF // 2)])
        for t in range(HALF)
    ]


def apply_odd(q):
    def at(index):
        index %= INST
        return q[index] if index < HALF else -q[index - HALF]

    def pair(t, m):
        low, high = (t - m) % INST, (t + m) % INST
        first = q[low % HALF] if low < HALF else None
        second = q[high % HALF] if high < HALF else None
        a, b = q[low % HALF], q[high % HALF]
        if first is not None and second is not None:
            return a - b, 1.0
        if first is None and second is not None:
            return a + b, -1.0
        if first is not None:
            return a + b, 1.0
        return a - b, -1.0

    result = []
    for t in range(HALF):
        terms = []
        for m in range(1, HALF // 2):
            value, sign = pair(t, m)
            terms.append((sign * ODD[m], value))
        last = (t - HALF // 2) % INST
        terms.append((ODD[HALF // 2] if last < HALF else -ODD[HALF // 2], q[last % HALF]))
        result.append(weighted(terms))
    return result


def row_shifts(tile, before, after):
    rows = tile.shape[0]
    row = lax.broadcasted_iota(jnp.int32, tile.shape, 0)
    following = jnp.where(row == rows - 1, after, pltpu.roll(tile, rows - 1, 0))
    previous = jnp.where(row == 0, before, pltpu.roll(tile, 1, 0))
    return following, previous


def east_west(tile):
    return pltpu.roll(tile, CELLS - 1, 1), pltpu.roll(tile, 1, 1)


def fetched(sources, held, ready):
    copies = [pltpu.make_async_copy(a, b, ready.at[k]) for k, (a, b) in enumerate(zip(sources, held))]
    for copy in copies:
        copy.start()
    return copies


def pack_kernel(live_in, state_ref, chunks_ref, faces_ref, live_ref, arrived, ready):
    first = lax.axis_index("blk") * BLOCKS
    scalars = fetched([live_in], [live_ref], ready)
    copies = []
    for i in range(INST):
        b, low = i // PER_BLOCK, (i % PER_BLOCK) * SLAB
        copy = pltpu.make_async_copy(
            state_ref.at[0, :, b, low : low + SLAB, :], chunks_ref.at[i, 0:VARS], arrived.at[i]
        )
        copy.start()
        copies.append(copy)
    for copy in copies + scalars:
        copy.wait()

    def row_of(v, b, row):
        return chunks_ref[b * PER_BLOCK + row // SLAB, v, pl.ds(row % SLAB, 1), :]

    for b in range(BLOCKS):
        last = live_ref[first + b] - 1
        for v in range(VARS):
            low, high = (2 * b) * VARS + v, (2 * b + 1) * VARS + v
            faces_ref[low : low + 1, :] = row_of(v, b, 0)
            faces_ref[high : high + 1, :] = row_of(v, b, last)
    faces = faces_ref[...]
    chunks_ref[0, VARS, 2 * VARS :, :] = faces[: SLAB - 2 * VARS, :]
    chunks_ref[0, VARS + 1, : FACES * VARS + 2 * VARS - SLAB, :] = faces[SLAB - 2 * VARS :, :]
    chunks_ref[0, VARS + 1, FACES * VARS + 2 * VARS - SLAB :, :] = jnp.zeros((SENT - FACE - FACES * VARS, CELLS), jnp.float32)
    chunks_ref[0, VARS, 0 : 2 * VARS, :] = jnp.zeros((2 * VARS, CELLS), jnp.float32)
    extra = chunks_ref[0, VARS : VARS + 2, :, :]
    for i in range(1, INST):
        chunks_ref[i, VARS : VARS + 2, :, :] = extra
    for i in range(INST):
        b, j = i // PER_BLOCK, i % PER_BLOCK
        for v in range(VARS):
            if j > 0:
                chunks_ref[i, VARS, v : v + 1, :] = row_of(v, b, j * SLAB - 1)
            if j < PER_BLOCK - 1:
                chunks_ref[i, VARS, VARS + v : VARS + v + 1, :] = row_of(v, b, (j + 1) * SLAB)


def ghost_place(partner_ref, face):
    me = lax.axis_index("blk")
    other = partner_ref[me * FACES + face]
    device, local = other // FACES, other % FACES
    core = (device % 2 + me % 2) % 2
    x = ((device // 2) % 4 - (me // 2) % 4 + 4) % 4
    y = (device // 8 + me // 8) % 2
    return (core * 4 + x) * 2 + y, local


def spatial_kernel(live_ref, partner_ref, row_ref, cell_ref, state_ref, visc_ref, step_ref, gathered_ref,
                   spatial_ref, faces_ref, half_ref):
    first = lax.axis_index("blk") * BLOCKS

    def stencil(tiles, befores, afters, mask_n, mask_p, damp):
        across, along, smooth = [], [], []
        for v in range(VARS):
            n, p = row_shifts(tiles[v], befores[v], afters[v])
            n, p = n * mask_n, p * mask_p
            e, w = east_west(tiles[v])
            across.append(n - p)
            along.append(e - w)
            smooth.append((n + p) + (e + w) - 4.0 * tiles[v])
        result = []
        for u in range(VARS):
            total = -damp * smooth[u]
            for v in range(VARS):
                total = total + (0.5 * row_ref[u, v]) * across[v] + (0.5 * cell_ref[u, v]) * along[v]
            result.append(total)
        return result

    def sweep(read, write, b, live):
        def step(j, carry):
            low = pl.multiple_of(j * SLAB, SLAB)
            before, after = jnp.maximum(low - 1, 0), jnp.minimum(low + SLAB, ROWS - 1)
            row = low + lax.broadcasted_iota(jnp.int32, (SLAB, CELLS), 0)
            mask_n = jnp.where(row + 1 < live, 1.0, 0.0)
            mask_p = jnp.where(row > 0, 1.0, 0.0)
            damp = 0.25 + visc_ref[b, pl.ds(low, SLAB), :]
            tiles = [read(v, b, pl.ds(low, SLAB)) for v in range(VARS)]
            befores = [read(v, b, pl.ds(before, 1)) for v in range(VARS)]
            afters = [read(v, b, pl.ds(after, 1)) for v in range(VARS)]
            result = stencil(tiles, befores, afters, mask_n, mask_p, damp)
            write(b, low, tiles, result)
            return carry

        lax.fori_loop(0, PER_BLOCK, step, 0)

    def read_state(v, b, rows):
        return state_ref[0, v, b, rows, :]

    def read_half(v, b, rows):
        return half_ref[v, b, rows, :]

    def write_half(b, low, tiles, result):
        scale = 0.5 * step_ref[b, pl.ds(low, SLAB), :]
        for v in range(VARS):
            half_ref[v, b, pl.ds(low, SLAB), :] = tiles[v] - scale * result[v]

    def write_spatial(b, low, tiles, result):
        for v in range(VARS):
            spatial_ref[v, b, pl.ds(low, SLAB), :] = result[v]

    for b in range(BLOCKS):
        live = live_ref[first + b]
        sweep(read_state, write_half, b, live)
        for side in range(2):
            place, local = ghost_place(partner_ref, 2 * b + side)
            row = (live - 1) if side else 0
            sign = 0.5 if side else -0.5
            rows = pl.ds(row, 1)
            ghost = [gathered_ref[place, pl.ds(local * VARS + v, 1), :] for v in range(VARS)]
            damp = 0.25 + visc_ref[b, rows, :]
            scale = 0.5 * step_ref[b, rows, :]
            for u in range(VARS):
                total = -damp * ghost[u]
                for v in range(VARS):
                    total = total + (sign * row_ref[u, v]) * ghost[v]
                half_ref[u, b, rows, :] = half_ref[u, b, rows, :] - scale * total
        for side in range(2):
            row = (live - 1) if side else 0
            for v in range(VARS):
                faces_ref[pl.ds((2 * b + side) * VARS + v, 1), :] = half_ref[v, b, pl.ds(row, 1), :]
        sweep(read_half, write_spatial, b, live)


def slab_kernel(live_in, row_in, cell_in, got_ref, visc_ref, step_ref, sent_ref, rate_ref, live_ref, row_ref, cell_ref, ready):
    scalars = fetched([live_in, row_in, cell_in], [live_ref, row_ref, cell_ref], ready)
    i = lax.axis_index("inst")
    b, j = i // PER_BLOCK, i % PER_BLOCK
    low = pl.multiple_of(j * SLAB, SLAB)
    step = step_ref[b, pl.ds(low, SLAB), :]

    def times(rows, with_second):
        values = [got_ref[t, rows, :] for t in range(INST)]
        p = [values[t] + values[t + HALF] for t in range(HALF)]
        q = [values[t] - values[t + HALF] for t in range(HALF)]
        p, q = apply_even(p), apply_odd(q)
        for t in range(HALF):
            rate_ref[t, rows, :] = p[t] + q[t]
            rate_ref[t + HALF, rows, :] = p[t] - q[t]
        if with_second is not None:
            p, q = apply_even(p), apply_odd(q)
            for t in range(HALF):
                sent_ref[t, rows, :] = with_second * (p[t] + q[t])
                sent_ref[t + HALF, rows, :] = with_second * (p[t] - q[t])

    half_step = [-step[0:8, :], -step[8:16, :]]
    for v in range(VARS):
        for k in range(2):
            at = v * SLAB + 8 * k
            times(slice(at, at + 8), half_step[k])
    times(slice(MAIN, MAIN + 8), None)
    times(slice(MAIN + 8, MAIN + 16), None)
    for copy in scalars:
        copy.wait()
    live = live_ref[lax.axis_index("blk") * BLOCKS + b]
    step_before = step_ref[b, pl.ds(jnp.maximum(low - 1, 0), 1), :]
    step_after = step_ref[b, pl.ds(jnp.minimum(low + SLAB, ROWS - 1), 1), :]
    row = low + lax.broadcasted_iota(jnp.int32, (SLAB, CELLS), 0)
    step_n, step_p = row_shifts(step, step_before, step_after)
    step_e, step_w = east_west(step)
    scale_n = jnp.where(row + 1 < live, step + step_n, 0.0)
    scale_p = jnp.where(row > 0, step + step_p, 0.0)
    scale_e, scale_w = step + step_e, step + step_w
    damp = 0.5 * (0.25 + visc_ref[b, pl.ds(low, SLAB), :])
    centre = 8.0 * step

    def instance(t, carry):
        across, along, smooth, rates = [], [], [], []
        for v in range(VARS):
            rate = rate_ref[t, pl.ds(v * SLAB, SLAB), :]
            n, p = row_shifts(rate, rate_ref[t, PREV + v : PREV + v + 1, :], rate_ref[t, NEXT + v : NEXT + v + 1, :])
            e, w = east_west(rate)
            n, p, e, w = scale_n * n, scale_p * p, scale_e * e, scale_w * w
            across.append(n - p)
            along.append(e - w)
            smooth.append((n + p) + (e + w) - centre * rate)
            rates.append(rate)
        for u in range(VARS):
            rows = pl.ds(u * SLAB, SLAB)
            total = sent_ref[t, rows, :] + rates[u] + damp * smooth[u]
            for v in range(VARS):
                total = total - (0.25 * row_ref[u, v]) * across[v] - (0.25 * cell_ref[u, v]) * along[v]
            sent_ref[t, rows, :] = total
        return carry

    lax.fori_loop(0, INST, instance, 0, unroll=4)


def face_kernel(live_ref, weights_ref, got_ref, half_ref, step_ref, out_ref):
    first = lax.axis_index("blk") * BLOCKS
    me = lax.axis_index("inst")
    total = jnp.zeros((FACES * VARS, CELLS), jnp.float32)
    for s in range(INST):
        total = total + weights_ref[me, s] * got_ref[s, FACE : FACE + FACES * VARS, :]
    out_ref[FACES * VARS :, :] = total
    for b in range(BLOCKS):
        for side in range(2):
            row = (live_ref[first + b] - 1) if side else 0
            scale = 0.5 * step_ref[b, pl.ds(row, 1), :]
            at = (2 * b + side) * VARS
            out_ref[at : at + VARS, :] = half_ref[at : at + VARS, :] - scale * total[at : at + VARS, :]


def final_kernel(live_in, partner_in, row_in, state_ref, visc_ref, step_ref, spatial_ref, got_ref, gathered_ref,
                 new_out, residual_out, new_ref, residual_ref, written, live_ref, partner_ref, row_ref, ready):
    for copy in fetched([live_in, partner_in, row_in], [live_ref, partner_ref, row_ref], ready):
        copy.wait()
    first = lax.axis_index("blk") * BLOCKS
    copies = []
    for b in range(BLOCKS):
        live = live_ref[first + b]
        for j in range(PER_BLOCK):
            low = j * SLAB
            rows = slice(low, low + SLAB)
            row = low + lax.broadcasted_iota(jnp.int32, (SLAB, CELLS), 0)
            step = step_ref[b, rows, :]
            for v in range(VARS):
                total = got_ref[b * PER_BLOCK + j, v * SLAB : (v + 1) * SLAB, :] + spatial_ref[v, b, rows, :]
                total = jnp.where(row < live, total, 0.0)
                residual_ref[v, b, rows, :] = total
                new_ref[v, b, rows, :] = state_ref[0, v, b, rows, :] - step * total
        for side in range(2):
            place, local = ghost_place(partner_ref, 2 * b + side)
            row = (live - 1) if side else 0
            sign = 0.5 if side else -0.5
            rows = pl.ds(row, 1)
            step = step_ref[b, rows, :]
            damp = 0.25 + visc_ref[b, rows, :]
            ghost = [
                gathered_ref[place, pl.ds(local * VARS + v, 1), :]
                - 0.5 * step * gathered_ref[place, pl.ds((FACES + local) * VARS + v, 1), :]
                for v in range(VARS)
            ]
            for u in range(VARS):
                total = -damp * ghost[u]
                for v in range(VARS):
                    total = total + (sign * row_ref[u, v]) * ghost[v]
                residual_ref[u, b, rows, :] = residual_ref[u, b, rows, :] + total
                new_ref[u, b, rows, :] = new_ref[u, b, rows, :] - step * total
        for k, (held, out) in enumerate(((new_ref, new_out), (residual_ref, residual_out))):
            copy = pltpu.make_async_copy(held.at[:, b], out.at[0, :, b], written.at[2 * b + k])
            copy.start()
            copies.append(copy)
    for copy in copies:
        copy.wait()


def call(body, outs, in_specs, scratch=(), name=None, out_specs=None, limit=32):
    return pl.pallas_call(
        body,
        out_shape=[jax.ShapeDtypeStruct(shape, jnp.float32) for shape in outs],
        in_specs=in_specs,
        out_specs=out_specs or [VMEM] * len(outs),
        scratch_shapes=list(scratch),
        compiler_params=pltpu.CompilerParams(vmem_limit_bytes=limit * 1024 * 1024),
        name=name,
    )


def gathered_over_blocks(value):
    def moved(array, y, x, core):
        pairs = []
        for to in range(16):
            source = ((to // 8 + y) % 2) * 8 + (((to // 2) % 4 + x) % 4) * 2 + (to + core) % 2
            pairs.append((source, to))
        return lax.ppermute(array, "blk", pairs)

    value = value[None]
    value = jnp.concatenate([value, moved(value, 1, 0, 0)])
    value = jnp.concatenate([value] + [moved(value, 0, x, 0) for x in (1, 2, 3)])
    return jnp.concatenate([value, moved(value, 0, 0, 1)])


def per_device(state, row_jacobian, cell_jacobian, viscosity, local_step, live_rows, partner):
    whole = state.shape
    chunks, faces = call(
        pack_kernel, [(INST, SENT // SLAB, SLAB, CELLS), (FACES * VARS, CELLS)], [HBM, HBM],
        [LIVE, pltpu.SemaphoreType.DMA((INST,)), pltpu.SemaphoreType.DMA((1,))], name="pack", limit=60
    )(live_rows, state)
    slabs = lax.all_to_all(chunks, "inst", 0, 0, tiled=True).reshape(INST, SENT, CELLS)
    ghosts = gathered_over_blocks(faces)
    spatial, half_faces = call(
        spatial_kernel,
        [(VARS, BLOCKS, ROWS, CELLS), (FACES * VARS, CELLS)],
        [SMEM, SMEM, SMEM, SMEM, VMEM, VMEM, VMEM, VMEM],
        [pltpu.VMEM((VARS, BLOCKS, ROWS, CELLS), jnp.float32)],
        name="spatial",
    )(live_rows, partner, row_jacobian, cell_jacobian, state, viscosity, local_step, ghosts)
    slabs, spatial = lax.optimization_barrier((slabs, spatial))
    (sent,) = call(
        slab_kernel, [(INST, MAIN, CELLS)], [HBM, HBM, HBM, VMEM, VMEM, VMEM],
        [pltpu.VMEM((INST, 96, CELLS), jnp.float32), LIVE, JACOBIAN, JACOBIAN, pltpu.SemaphoreType.DMA((3,))], name="slab"
    )(live_rows, row_jacobian, cell_jacobian, slabs, viscosity, local_step)
    back = lax.all_to_all(sent, "inst", 0, 0, tiled=True)
    weights = jnp.array([[spectral(t - s) for s in range(INST)] for t in range(INST)], jnp.float32)
    (faces2,) = call(
        face_kernel, [(2 * FACES * VARS, CELLS)], [SMEM, SMEM, VMEM, VMEM, VMEM], name="faces"
    )(live_rows, weights, slabs, half_faces, local_step)
    ghosts2 = gathered_over_blocks(faces2)
    new_state, residual = call(
        final_kernel, [whole, whole], [HBM, HBM, HBM] + [VMEM] * 6,
        [pltpu.VMEM((VARS, BLOCKS, ROWS, CELLS), jnp.float32)] * 2
        + [pltpu.SemaphoreType.DMA((2 * BLOCKS,)), LIVE, PARTNER, JACOBIAN, pltpu.SemaphoreType.DMA((3,))],
        name="final", out_specs=[HBM] * 2
    )(live_rows, partner, row_jacobian, state, viscosity, local_step, spatial, back, ghosts2)
    return new_state, residual


def solution(mesh):
    return jax.shard_map(
        per_device,
        mesh=mesh,
        in_specs=(
            P("inst", None, "blk", None, None),
            P(),
            P(),
            P("blk", None, None),
            P("blk", None, None),
            P(),
            P(),
        ),
        out_specs=(P("inst", None, "blk", None, None), P("inst", None, "blk", None, None)),
        check_vma=False,
    )
```

```python
import itertools
import math

import jax
import jax.numpy as jnp
from jax import lax
from jax.experimental import pallas as pl
from jax.experimental.pallas import tpu as pltpu
from jax.sharding import PartitionSpec as P

VARS, BLOCKS, ROWS, CELLS, INST = 5, 2, 128, 128, 16
SLAB = 16
PER_BLOCK = ROWS // SLAB
MAIN = VARS * SLAB
PREV, NEXT, FACE = MAIN, MAIN + VARS, MAIN + 2 * VARS
SENT = 112
FACES = 2 * BLOCKS
VMEM = pl.BlockSpec(memory_space=pltpu.VMEM)
SMEM = pl.BlockSpec(memory_space=pltpu.SMEM)
HBM = pl.BlockSpec(memory_space=pltpu.HBM)

SIZES = {"y": 2, "x": 4, "core": 2}
ORDER = (("y", "core",), ("x",),)
ORDER2 = (("y", "core",), ("x",),)
LIVE = pltpu.SMEM((32,), jnp.int32)
JACOBIAN = pltpu.SMEM((VARS, VARS), jnp.float32)


def spectral(m):
    m = m % INST
    if m in (0, INST // 2):
        return 0.0
    return 0.5 * (-1.0) ** m * math.cos(math.pi * m / INST) / math.sin(math.pi * m / INST)


HALF = INST // 2
EVEN = [0.5 * (spectral(m) + spectral(m + HALF)) for m in range(HALF)]
ODD = [0.5 * (spectral(m) - spectral(m + HALF)) for m in range(HALF)]


def weighted(terms):
    total = None
    for weight, value in terms:
        term = weight * value
        total = term if total is None else total + term
    return total


def apply_even(p):
    return [
        weighted([(EVEN[m], p[(t - m) % HALF] - p[(t + m) % HALF]) for m in range(1, HALF // 2)])
        for t in range(HALF)
    ]


def apply_odd(q):
    def at(index):
        index %= INST
        return q[index] if index < HALF else -q[index - HALF]

    def pair(t, m):
        low, high = (t - m) % INST, (t + m) % INST
        first = q[low % HALF] if low < HALF else None
        second = q[high % HALF] if high < HALF else None
        a, b = q[low % HALF], q[high % HALF]
        if first is not None and second is not None:
            return a - b, 1.0
        if first is None and second is not None:
            return a + b, -1.0
        if first is not None:
            return a + b, 1.0
        return a - b, -1.0

    result = []
    for t in range(HALF):
        terms = []
        for m in range(1, HALF // 2):
            value, sign = pair(t, m)
            terms.append((sign * ODD[m], value))
        last = (t - HALF // 2) % INST
        terms.append((ODD[HALF // 2] if last < HALF else -ODD[HALF // 2], q[last % HALF]))
        result.append(weighted(terms))
    return result


def row_shifts(tile, before, after):
    rows = tile.shape[0]
    row = lax.broadcasted_iota(jnp.int32, tile.shape, 0)
    following = jnp.where(row == rows - 1, after, pltpu.roll(tile, rows - 1, 0))
    previous = jnp.where(row == 0, before, pltpu.roll(tile, 1, 0))
    return following, previous


def east_west(tile):
    return pltpu.roll(tile, CELLS - 1, 1), pltpu.roll(tile, 1, 1)


def fetched(sources, held, ready):
    copies = [pltpu.make_async_copy(a, b, ready.at[k]) for k, (a, b) in enumerate(zip(sources, held))]
    for copy in copies:
        copy.start()
    return copies


def pack_kernel(live_in, state_ref, chunks_ref, faces_ref, live_ref, arrived, ready):
    first = lax.axis_index("blk") * BLOCKS
    scalars = fetched([live_in], [live_ref], ready)
    copies = []
    for i in range(INST):
        b, low = i // PER_BLOCK, (i % PER_BLOCK) * SLAB
        copy = pltpu.make_async_copy(
            state_ref.at[0, :, b, low : low + SLAB, :], chunks_ref.at[i, 0:VARS], arrived.at[i]
        )
        copy.start()
        copies.append(copy)
    for copy in copies + scalars:
        copy.wait()

    def row_of(v, b, row):
        return chunks_ref[b * PER_BLOCK + row // SLAB, v, pl.ds(row % SLAB, 1), :]

    for b in range(BLOCKS):
        last = live_ref[first + b] - 1
        for v in range(VARS):
            low, high = (2 * b) * VARS + v, (2 * b + 1) * VARS + v
            faces_ref[low : low + 1, :] = row_of(v, b, 0)
            faces_ref[high : high + 1, :] = row_of(v, b, last)
    faces = faces_ref[...]
    chunks_ref[0, VARS, 2 * VARS :, :] = faces[: SLAB - 2 * VARS, :]
    chunks_ref[0, VARS + 1, : FACES * VARS + 2 * VARS - SLAB, :] = faces[SLAB - 2 * VARS :, :]
    chunks_ref[0, VARS + 1, FACES * VARS + 2 * VARS - SLAB :, :] = jnp.zeros((SENT - FACE - FACES * VARS, CELLS), jnp.float32)
    chunks_ref[0, VARS, 0 : 2 * VARS, :] = jnp.zeros((2 * VARS, CELLS), jnp.float32)
    extra = chunks_ref[0, VARS : VARS + 2, :, :]
    for i in range(1, INST):
        chunks_ref[i, VARS : VARS + 2, :, :] = extra
    for i in range(INST):
        b, j = i // PER_BLOCK, i % PER_BLOCK
        for v in range(VARS):
            if j > 0:
                chunks_ref[i, VARS, v : v + 1, :] = row_of(v, b, j * SLAB - 1)
            if j < PER_BLOCK - 1:
                chunks_ref[i, VARS, VARS + v : VARS + v + 1, :] = row_of(v, b, (j + 1) * SLAB)


def ghost_place(partner_ref, face, order):
    me = lax.axis_index("blk")
    other = partner_ref[me * FACES + face]
    device, local = other // FACES, other % FACES
    away = {
        "core": (device % 2 + me % 2) % 2,
        "x": ((device // 2) % 4 - (me // 2) % 4 + 4) % 4,
        "y": (device // 8 + me // 8) % 2,
    }
    place = 0
    for stage in reversed(order):
        for axis in stage:
            place = place * SIZES[axis] + away[axis]
    return place, local


def spatial_kernel(live_ref, partner_ref, row_ref, cell_ref, state_ref, visc_ref, step_ref, gathered_ref,
                   spatial_ref, faces_ref, mask_ref, half_ref):
    first = lax.axis_index("blk") * BLOCKS

    def stencil(tiles, befores, afters, mask_n, mask_p, damp):
        across, along, smooth = [], [], []
        for v in range(VARS):
            n, p = row_shifts(tiles[v], befores[v], afters[v])
            n, p = n * mask_n, p * mask_p
            e, w = east_west(tiles[v])
            across.append(n - p)
            along.append(e - w)
            smooth.append((n + p) + (e + w) - 4.0 * tiles[v])
        result = []
        for u in range(VARS):
            total = -damp * smooth[u]
            for v in range(VARS):
                total = total + (0.5 * row_ref[u, v]) * across[v] + (0.5 * cell_ref[u, v]) * along[v]
            result.append(total)
        return result

    def sweep(read, write, b, live):
        def step(j, carry):
            low = pl.multiple_of(j * SLAB, SLAB)
            before, after = jnp.maximum(low - 1, 0), jnp.minimum(low + SLAB, ROWS - 1)
            row = low + lax.broadcasted_iota(jnp.int32, (SLAB, CELLS), 0)
            mask_n = jnp.where(row + 1 < live, 1.0, 0.0)
            mask_p = jnp.where(row > 0, 1.0, 0.0)
            damp = 0.25 + visc_ref[b, pl.ds(low, SLAB), :]
            tiles = [read(v, b, pl.ds(low, SLAB)) for v in range(VARS)]
            befores = [read(v, b, pl.ds(before, 1)) for v in range(VARS)]
            afters = [read(v, b, pl.ds(after, 1)) for v in range(VARS)]
            result = stencil(tiles, befores, afters, mask_n, mask_p, damp)
            write(b, low, tiles, result)
            return carry

        lax.fori_loop(0, PER_BLOCK, step, 0)

    def read_state(v, b, rows):
        return state_ref[0, v, b, rows, :]

    def read_half(v, b, rows):
        return half_ref[v, b, rows, :]

    def write_half(b, low, tiles, result):
        scale = 0.5 * step_ref[b, pl.ds(low, SLAB), :]
        for v in range(VARS):
            half_ref[v, b, pl.ds(low, SLAB), :] = tiles[v] - scale * result[v]

    def write_spatial(b, low, tiles, result):
        row = low + lax.broadcasted_iota(jnp.int32, (SLAB, CELLS), 0)
        inside = row < live_ref[first + b]
        mask_ref[b, pl.ds(low, SLAB), :] = jnp.where(inside, 1.0, 0.0)
        for v in range(VARS):
            spatial_ref[v, b, pl.ds(low, SLAB), :] = jnp.where(inside, result[v], 0.0)

    for b in range(BLOCKS):
        live = live_ref[first + b]
        sweep(read_state, write_half, b, live)
        for side in range(2):
            place, local = ghost_place(partner_ref, 2 * b + side, ORDER)
            row = (live - 1) if side else 0
            sign = 0.5 if side else -0.5
            rows = pl.ds(row, 1)
            ghost = [gathered_ref[place, pl.ds(local * VARS + v, 1), :] for v in range(VARS)]
            damp = 0.25 + visc_ref[b, rows, :]
            scale = 0.5 * step_ref[b, rows, :]
            for u in range(VARS):
                total = -damp * ghost[u]
                for v in range(VARS):
                    total = total + (sign * row_ref[u, v]) * ghost[v]
                half_ref[u, b, rows, :] = half_ref[u, b, rows, :] - scale * total
        for side in range(2):
            row = (live - 1) if side else 0
            for v in range(VARS):
                faces_ref[pl.ds((2 * b + side) * VARS + v, 1), :] = half_ref[v, b, pl.ds(row, 1), :]
        sweep(read_half, write_spatial, b, live)


def slab_kernel(live_in, row_in, cell_in, got_ref, visc_ref, step_ref, out_ref, sent_ref, rate_ref, live_ref, row_ref, cell_ref, ready, written):
    scalars = fetched([live_in, row_in, cell_in], [live_ref, row_ref, cell_ref], ready)
    i = lax.axis_index("inst")
    b, j = i // PER_BLOCK, i % PER_BLOCK
    low = pl.multiple_of(j * SLAB, SLAB)
    step = step_ref[b, pl.ds(low, SLAB), :]

    def times(rows, with_second):
        values = [got_ref[t, rows, :] for t in range(INST)]
        p = [values[t] + values[t + HALF] for t in range(HALF)]
        q = [values[t] - values[t + HALF] for t in range(HALF)]
        p, q = apply_even(p), apply_odd(q)
        for t in range(HALF):
            rate_ref[t, rows, :] = p[t] + q[t]
            rate_ref[t + HALF, rows, :] = p[t] - q[t]
        if with_second is not None:
            p, q = apply_even(p), apply_odd(q)
            for t in range(HALF):
                sent_ref[t, rows, :] = with_second * (p[t] + q[t])
                sent_ref[t + HALF, rows, :] = with_second * (p[t] - q[t])

    half_step = [-step[0:8, :], -step[8:16, :]]
    for v in range(VARS):
        for k in range(2):
            at = v * SLAB + 8 * k
            times(slice(at, at + 8), half_step[k])
    times(slice(MAIN, MAIN + 8), None)
    times(slice(MAIN + 8, MAIN + 16), None)
    for copy in scalars:
        copy.wait()
    live = live_ref[lax.axis_index("blk") * BLOCKS + b]
    step_before = step_ref[b, pl.ds(jnp.maximum(low - 1, 0), 1), :]
    step_after = step_ref[b, pl.ds(jnp.minimum(low + SLAB, ROWS - 1), 1), :]
    row = low + lax.broadcasted_iota(jnp.int32, (SLAB, CELLS), 0)
    step_n, step_p = row_shifts(step, step_before, step_after)
    step_e, step_w = east_west(step)
    scale_n = jnp.where(row + 1 < live, step + step_n, 0.0)
    scale_p = jnp.where(row > 0, step + step_p, 0.0)
    scale_e, scale_w = step + step_e, step + step_w
    damp = 0.5 * (0.25 + visc_ref[b, pl.ds(low, SLAB), :])
    centre = 1.0 - 8.0 * step * damp

    def spread(coefficients):
        return [[jnp.full((SLAB, CELLS), 0.25 * coefficients[u, v]) for v in range(VARS)] for u in range(VARS)]

    scale_row, scale_cell = spread(row_ref), spread(cell_ref)

    def instance(t, carry):
        across, along, smooth = [], [], []
        for v in range(VARS):
            rate = rate_ref[t, pl.ds(v * SLAB, SLAB), :]
            n, p = row_shifts(rate, rate_ref[t, PREV + v : PREV + v + 1, :], rate_ref[t, NEXT + v : NEXT + v + 1, :])
            e, w = east_west(rate)
            n, p, e, w = scale_n * n, scale_p * p, scale_e * e, scale_w * w
            across.append(n - p)
            along.append(e - w)
            smooth.append(centre * rate + damp * ((n + p) + (e + w)))
        for u in range(VARS):
            rows = pl.ds(u * SLAB, SLAB)
            total = sent_ref[t, rows, :] + smooth[u]
            for v in range(VARS):
                total = total - scale_row[u][v] * across[v] - scale_cell[u][v] * along[v]
            sent_ref[t, rows, :] = total
        return carry

    lax.fori_loop(0, INST, instance, 0, unroll=4)
    copy = pltpu.make_async_copy(sent_ref, out_ref, written.at[0])
    copy.start()
    copy.wait()


def face_kernel(live_ref, weights_ref, got_ref, half_ref, step_ref, out_ref):
    first = lax.axis_index("blk") * BLOCKS
    me = lax.axis_index("inst")
    total = jnp.zeros((FACES * VARS, CELLS), jnp.float32)
    for s in range(INST):
        total = total + weights_ref[me, s] * got_ref[s, FACE : FACE + FACES * VARS, :]
    out_ref[FACES * VARS :, :] = total
    for b in range(BLOCKS):
        for side in range(2):
            row = (live_ref[first + b] - 1) if side else 0
            scale = 0.5 * step_ref[b, pl.ds(row, 1), :]
            at = (2 * b + side) * VARS
            out_ref[at : at + VARS, :] = half_ref[at : at + VARS, :] - scale * total[at : at + VARS, :]


def ghost_kernel(live_ref, partner_ref, row_ref, visc_ref, step_ref, gathered_ref, spatial_in, spatial_ref):
    del spatial_in
    first = lax.axis_index("blk") * BLOCKS
    for b in range(BLOCKS):
        for side in range(2):
            place, local = ghost_place(partner_ref, 2 * b + side, ORDER2)
            row = (live_ref[first + b] - 1) if side else 0
            sign = 0.5 if side else -0.5
            rows = pl.ds(row, 1)
            step = step_ref[b, rows, :]
            damp = 0.25 + visc_ref[b, rows, :]
            ghost = [
                gathered_ref[place, pl.ds(local * VARS + v, 1), :]
                - 0.5 * step * gathered_ref[place, pl.ds((FACES + local) * VARS + v, 1), :]
                for v in range(VARS)
            ]
            for u in range(VARS):
                total = -damp * ghost[u]
                for v in range(VARS):
                    total = total + (sign * row_ref[u, v]) * ghost[v]
                spatial_ref[u, b, rows, :] = spatial_ref[u, b, rows, :] + total


def final_kernel(state_ref, step_ref, mask_ref, spatial_ref, got_ref, new_out, residual_out, new_ref, residual_ref, written):
    copies = []
    for b in range(BLOCKS):

        def tile(j, carry):
            rows = pl.ds(pl.multiple_of(j * SLAB, SLAB), SLAB)
            step, mask = step_ref[b, rows, :], mask_ref[b, rows, :]
            for v in range(VARS):
                total = mask * got_ref[b * PER_BLOCK + j, v * SLAB : (v + 1) * SLAB, :] + spatial_ref[v, b, rows, :]
                residual_ref[v, b, rows, :] = total
                new_ref[v, b, rows, :] = state_ref[0, v, b, rows, :] - step * total
            return carry

        lax.fori_loop(0, PER_BLOCK, tile, 0, unroll=2)
        for k, (held, out) in enumerate(((new_ref, new_out), (residual_ref, residual_out))):
            copy = pltpu.make_async_copy(held.at[:, b], out.at[0, :, b], written.at[2 * b + k])
            copy.start()
            copies.append(copy)
    for copy in copies:
        copy.wait()


def call(body, outs, in_specs, scratch=(), name=None, out_specs=None, limit=32, aliases=None):
    return pl.pallas_call(
        body,
        out_shape=[jax.ShapeDtypeStruct(shape, jnp.float32) for shape in outs],
        in_specs=in_specs,
        out_specs=out_specs or [VMEM] * len(outs),
        scratch_shapes=list(scratch),
        compiler_params=pltpu.CompilerParams(vmem_limit_bytes=limit * 1024 * 1024),
        input_output_aliases=aliases or {},
        name=name,
    )


def gathered_over_blocks(value, order):
    def moved(array, y=0, x=0, core=0):
        pairs = []
        for to in range(16):
            source = ((to // 8 + y) % 2) * 8 + (((to // 2) % 4 + x) % 4) * 2 + (to + core) % 2
            pairs.append((source, to))
        return lax.ppermute(array, "blk", pairs)

    value = value[None]
    for stage in order:
        steps = itertools.product(*(range(SIZES[axis]) for axis in stage))
        moves = [moved(value, **dict(zip(stage, step))) for step in list(steps)[1:]]
        value = jnp.concatenate([value] + moves)
    return value


def per_device(state, row_jacobian, cell_jacobian, viscosity, local_step, live_rows, partner):
    whole = state.shape
    chunks, faces = call(
        pack_kernel, [(INST, SENT // SLAB, SLAB, CELLS), (FACES * VARS, CELLS)], [HBM, HBM],
        [LIVE, pltpu.SemaphoreType.DMA((INST,)), pltpu.SemaphoreType.DMA((1,))], name="pack", limit=60
    )(live_rows, state)
    slabs = lax.all_to_all(chunks, "inst", 0, 0, tiled=True).reshape(INST, SENT, CELLS)
    ghosts = gathered_over_blocks(faces, ORDER)
    spatial, half_faces, mask = call(
        spatial_kernel,
        [(VARS, BLOCKS, ROWS, CELLS), (FACES * VARS, CELLS), (BLOCKS, ROWS, CELLS)],
        [SMEM, SMEM, SMEM, SMEM, VMEM, VMEM, VMEM, VMEM],
        [pltpu.VMEM((VARS, BLOCKS, ROWS, CELLS), jnp.float32)],
        name="spatial",
    )(live_rows, partner, row_jacobian, cell_jacobian, state, viscosity, local_step, ghosts)
    slabs, spatial = lax.optimization_barrier((slabs, spatial))
    (sent,) = call(
        slab_kernel, [(INST, MAIN, CELLS)], [HBM, HBM, HBM, VMEM, VMEM, VMEM],
        [
            pltpu.VMEM((INST, MAIN, CELLS), jnp.float32),
            pltpu.VMEM((INST, 96, CELLS), jnp.float32),
            LIVE,
            JACOBIAN,
            JACOBIAN,
            pltpu.SemaphoreType.DMA((3,)),
            pltpu.SemaphoreType.DMA((1,)),
        ],
        name="slab", out_specs=[HBM],
    )(live_rows, row_jacobian, cell_jacobian, slabs, viscosity, local_step)
    back = lax.all_to_all(sent, "inst", 0, 0, tiled=True)
    weights = jnp.array([[spectral(t - s) for s in range(INST)] for t in range(INST)], jnp.float32)
    (faces2,) = call(
        face_kernel, [(2 * FACES * VARS, CELLS)], [SMEM, SMEM, VMEM, VMEM, VMEM], name="faces"
    )(live_rows, weights, slabs, half_faces, local_step)
    ghosts2 = gathered_over_blocks(faces2, ORDER2)
    (spatial,) = call(
        ghost_kernel, [(VARS, BLOCKS, ROWS, CELLS)], [SMEM, SMEM, SMEM] + [VMEM] * 4, name="ghosts", aliases={6: 0}
    )(live_rows, partner, row_jacobian, viscosity, local_step, ghosts2, spatial)
    new_state, residual = call(
        final_kernel, [whole, whole], [VMEM] * 5,
        [pltpu.VMEM((VARS, BLOCKS, ROWS, CELLS), jnp.float32)] * 2 + [pltpu.SemaphoreType.DMA((2 * BLOCKS,))],
        name="final", out_specs=[HBM] * 2,
    )(state, local_step, mask, spatial, back)
    return new_state, residual


def solution(mesh):
    return jax.shard_map(
        per_device,
        mesh=mesh,
        in_specs=(
            P("inst", None, "blk", None, None),
            P(),
            P(),
            P("blk", None, None),
            P("blk", None, None),
            P(),
            P(),
        ),
        out_specs=(P("inst", None, "blk", None, None), P("inst", None, "blk", None, None)),
        check_vma=False,
    )
```

```python
import itertools
import math

import jax
import jax.numpy as jnp
from jax import lax
from jax.experimental import pallas as pl
from jax.experimental.pallas import tpu as pltpu
from jax.sharding import PartitionSpec as P

VARS, BLOCKS, ROWS, CELLS, INST = 5, 2, 128, 128, 16
SLAB = 16
PER_BLOCK = ROWS // SLAB
MAIN = VARS * SLAB
PREV, NEXT, FACE = MAIN, MAIN + VARS, MAIN + 2 * VARS
SENT = 112
FACES = 2 * BLOCKS
VMEM = pl.BlockSpec(memory_space=pltpu.VMEM)
SMEM = pl.BlockSpec(memory_space=pltpu.SMEM)
HBM = pl.BlockSpec(memory_space=pltpu.HBM)

SIZES = {"y": 2, "x": 4, "core": 2}
ORDER = (("y", "core",), ("x",),)
ORDER2 = (("y", "core",), ("x",),)
LIVE = pltpu.SMEM((32,), jnp.int32)
JACOBIAN = pltpu.SMEM((VARS, VARS), jnp.float32)


def spectral(m):
    m = m % INST
    if m in (0, INST // 2):
        return 0.0
    return 0.5 * (-1.0) ** m * math.cos(math.pi * m / INST) / math.sin(math.pi * m / INST)


HALF = INST // 2
GROUP = 4
EVEN = [0.5 * (spectral(m) + spectral(m + HALF)) for m in range(HALF)]
ODD = [0.5 * (spectral(m) - spectral(m + HALF)) for m in range(HALF)]


def weighted(terms):
    total = None
    for weight, value in terms:
        term = weight * value
        total = term if total is None else total + term
    return total


def apply_even(p):
    return [
        weighted([(EVEN[m], p[(t - m) % HALF] - p[(t + m) % HALF]) for m in range(1, HALF // 2)])
        for t in range(HALF)
    ]


def apply_odd(q):
    def at(index):
        index %= INST
        return q[index] if index < HALF else -q[index - HALF]

    def pair(t, m):
        low, high = (t - m) % INST, (t + m) % INST
        first = q[low % HALF] if low < HALF else None
        second = q[high % HALF] if high < HALF else None
        a, b = q[low % HALF], q[high % HALF]
        if first is not None and second is not None:
            return a - b, 1.0
        if first is None and second is not None:
            return a + b, -1.0
        if first is not None:
            return a + b, 1.0
        return a - b, -1.0

    result = []
    for t in range(HALF):
        terms = []
        for m in range(1, HALF // 2):
            value, sign = pair(t, m)
            terms.append((sign * ODD[m], value))
        last = (t - HALF // 2) % INST
        terms.append((ODD[HALF // 2] if last < HALF else -ODD[HALF // 2], q[last % HALF]))
        result.append(weighted(terms))
    return result


def row_shifts(tile, before, after):
    rows = tile.shape[0]
    row = lax.broadcasted_iota(jnp.int32, tile.shape, 0)
    following = jnp.where(row == rows - 1, after, pltpu.roll(tile, rows - 1, 0))
    previous = jnp.where(row == 0, before, pltpu.roll(tile, 1, 0))
    return following, previous


def east_west(tile):
    return pltpu.roll(tile, CELLS - 1, 1), pltpu.roll(tile, 1, 1)


def fetched(sources, held, ready):
    copies = [pltpu.make_async_copy(a, b, ready.at[k]) for k, (a, b) in enumerate(zip(sources, held))]
    for copy in copies:
        copy.start()
    return copies


def pack_kernel(live_in, state_ref, chunks_ref, faces_ref, live_ref, arrived, ready):
    first = lax.axis_index("blk") * BLOCKS
    scalars = fetched([live_in], [live_ref], ready)
    copies = []
    for i in range(INST):
        b, low = i // PER_BLOCK, (i % PER_BLOCK) * SLAB
        copy = pltpu.make_async_copy(
            state_ref.at[0, :, b, low : low + SLAB, :], chunks_ref.at[i, 0:VARS], arrived.at[i]
        )
        copy.start()
        copies.append(copy)
    for copy in copies + scalars:
        copy.wait()

    def row_of(v, b, row):
        return chunks_ref[b * PER_BLOCK + row // SLAB, v, pl.ds(row % SLAB, 1), :]

    for b in range(BLOCKS):
        last = live_ref[first + b] - 1
        for v in range(VARS):
            low, high = (2 * b) * VARS + v, (2 * b + 1) * VARS + v
            faces_ref[low : low + 1, :] = row_of(v, b, 0)
            faces_ref[high : high + 1, :] = row_of(v, b, last)
    faces = faces_ref[...]
    chunks_ref[0, VARS, 2 * VARS :, :] = faces[: SLAB - 2 * VARS, :]
    chunks_ref[0, VARS + 1, : FACES * VARS + 2 * VARS - SLAB, :] = faces[SLAB - 2 * VARS :, :]
    chunks_ref[0, VARS + 1, FACES * VARS + 2 * VARS - SLAB :, :] = jnp.zeros((SENT - FACE - FACES * VARS, CELLS), jnp.float32)
    chunks_ref[0, VARS, 0 : 2 * VARS, :] = jnp.zeros((2 * VARS, CELLS), jnp.float32)
    extra = chunks_ref[0, VARS : VARS + 2, :, :]
    for i in range(1, INST):
        chunks_ref[i, VARS : VARS + 2, :, :] = extra
    for i in range(INST):
        b, j = i // PER_BLOCK, i % PER_BLOCK
        for v in range(VARS):
            if j > 0:
                chunks_ref[i, VARS, v : v + 1, :] = row_of(v, b, j * SLAB - 1)
            if j < PER_BLOCK - 1:
                chunks_ref[i, VARS, VARS + v : VARS + v + 1, :] = row_of(v, b, (j + 1) * SLAB)


def ghost_place(partner_ref, face, order):
    me = lax.axis_index("blk")
    other = partner_ref[me * FACES + face]
    device, local = other // FACES, other % FACES
    away = {
        "core": (device % 2 + me % 2) % 2,
        "x": ((device // 2) % 4 - (me // 2) % 4 + 4) % 4,
        "y": (device // 8 + me // 8) % 2,
    }
    place = 0
    for stage in reversed(order):
        for axis in stage:
            place = place * SIZES[axis] + away[axis]
    return place, local


def spatial_kernel(live_ref, partner_ref, row_ref, cell_ref, state_ref, visc_ref, step_ref, gathered_ref,
                   spatial_ref, faces_ref, mask_ref, half_ref):
    first = lax.axis_index("blk") * BLOCKS

    def stencil(tiles, befores, afters, mask_n, mask_p, damp):
        across, along, smooth = [], [], []
        for v in range(VARS):
            n, p = row_shifts(tiles[v], befores[v], afters[v])
            n, p = n * mask_n, p * mask_p
            e, w = east_west(tiles[v])
            across.append(n - p)
            along.append(e - w)
            smooth.append((n + p) + (e + w) - 4.0 * tiles[v])
        result = []
        for u in range(VARS):
            total = -damp * smooth[u]
            for v in range(VARS):
                total = total + (0.5 * row_ref[u, v]) * across[v] + (0.5 * cell_ref[u, v]) * along[v]
            result.append(total)
        return result

    def sweep(read, write, b, live):
        def step(j, carry):
            low = pl.multiple_of(j * SLAB, SLAB)
            before, after = jnp.maximum(low - 1, 0), jnp.minimum(low + SLAB, ROWS - 1)
            row = low + lax.broadcasted_iota(jnp.int32, (SLAB, CELLS), 0)
            mask_n = jnp.where(row + 1 < live, 1.0, 0.0)
            mask_p = jnp.where(row > 0, 1.0, 0.0)
            damp = 0.25 + visc_ref[b, pl.ds(low, SLAB), :]
            tiles = [read(v, b, pl.ds(low, SLAB)) for v in range(VARS)]
            befores = [read(v, b, pl.ds(before, 1)) for v in range(VARS)]
            afters = [read(v, b, pl.ds(after, 1)) for v in range(VARS)]
            result = stencil(tiles, befores, afters, mask_n, mask_p, damp)
            write(b, low, tiles, result)
            return carry

        lax.fori_loop(0, PER_BLOCK, step, 0)

    def read_state(v, b, rows):
        return state_ref[0, v, b, rows, :]

    def read_half(v, b, rows):
        return half_ref[v, b, rows, :]

    def write_half(b, low, tiles, result):
        scale = 0.5 * step_ref[b, pl.ds(low, SLAB), :]
        for v in range(VARS):
            half_ref[v, b, pl.ds(low, SLAB), :] = tiles[v] - scale * result[v]

    def write_spatial(b, low, tiles, result):
        row = low + lax.broadcasted_iota(jnp.int32, (SLAB, CELLS), 0)
        inside = row < live_ref[first + b]
        mask_ref[b, pl.ds(low, SLAB), :] = jnp.where(inside, 1.0, 0.0)
        for v in range(VARS):
            spatial_ref[v, b, pl.ds(low, SLAB), :] = jnp.where(inside, result[v], 0.0)

    for b in range(BLOCKS):
        live = live_ref[first + b]
        sweep(read_state, write_half, b, live)
        for side in range(2):
            place, local = ghost_place(partner_ref, 2 * b + side, ORDER)
            row = (live - 1) if side else 0
            sign = 0.5 if side else -0.5
            rows = pl.ds(row, 1)
            ghost = [gathered_ref[place, pl.ds(local * VARS + v, 1), :] for v in range(VARS)]
            damp = 0.25 + visc_ref[b, rows, :]
            scale = 0.5 * step_ref[b, rows, :]
            for u in range(VARS):
                total = -damp * ghost[u]
                for v in range(VARS):
                    total = total + (sign * row_ref[u, v]) * ghost[v]
                half_ref[u, b, rows, :] = half_ref[u, b, rows, :] - scale * total
        for side in range(2):
            row = (live - 1) if side else 0
            for v in range(VARS):
                faces_ref[pl.ds((2 * b + side) * VARS + v, 1), :] = half_ref[v, b, pl.ds(row, 1), :]
        sweep(read_half, write_spatial, b, live)


def slab_kernel(live_in, row_in, cell_in, got_ref, visc_ref, step_ref, out_ref, sent_ref, rate_ref, live_ref, row_ref, cell_ref, ready, written):
    scalars = fetched([live_in, row_in, cell_in], [live_ref, row_ref, cell_ref], ready)
    i = lax.axis_index("inst")
    b, j = i // PER_BLOCK, i % PER_BLOCK
    low = pl.multiple_of(j * SLAB, SLAB)
    step = step_ref[b, pl.ds(low, SLAB), :]

    def times(rows, with_second):
        values = [got_ref[t, rows, :] for t in range(INST)]
        p = [values[t] + values[t + HALF] for t in range(HALF)]
        q = [values[t] - values[t + HALF] for t in range(HALF)]
        p, q = apply_even(p), apply_odd(q)
        for t in range(HALF):
            rate_ref[t, rows, :] = p[t] + q[t]
            rate_ref[t + HALF, rows, :] = p[t] - q[t]
        if with_second is not None:
            p, q = apply_even(p), apply_odd(q)
            for t in range(HALF):
                sent_ref[t, rows, :] = with_second * (p[t] + q[t])
                sent_ref[t + HALF, rows, :] = with_second * (p[t] - q[t])

    half_step = [-step[0:8, :], -step[8:16, :]]
    for v in range(VARS):
        for k in range(2):
            at = v * SLAB + 8 * k
            times(slice(at, at + 8), half_step[k])
    times(slice(MAIN, MAIN + 8), None)
    times(slice(MAIN + 8, MAIN + 16), None)
    for copy in scalars:
        copy.wait()
    live = live_ref[lax.axis_index("blk") * BLOCKS + b]
    step_before = step_ref[b, pl.ds(jnp.maximum(low - 1, 0), 1), :]
    step_after = step_ref[b, pl.ds(jnp.minimum(low + SLAB, ROWS - 1), 1), :]
    row = low + lax.broadcasted_iota(jnp.int32, (SLAB, CELLS), 0)
    step_n, step_p = row_shifts(step, step_before, step_after)
    step_e, step_w = east_west(step)
    scale_n = jnp.where(row + 1 < live, step + step_n, 0.0)
    scale_p = jnp.where(row > 0, step + step_p, 0.0)
    scale_e, scale_w = step + step_e, step + step_w
    damp = 0.5 * (0.25 + visc_ref[b, pl.ds(low, SLAB), :])
    centre = 1.0 - 8.0 * step * damp

    def spread(coefficients):
        return [[jnp.full((SLAB, CELLS), 0.25 * coefficients[u, v]) for v in range(VARS)] for u in range(VARS)]

    scale_row, scale_cell = spread(row_ref), spread(cell_ref)

    def instance(t, carry):
        across, along, smooth = [], [], []
        for v in range(VARS):
            rate = rate_ref[t, pl.ds(v * SLAB, SLAB), :]
            n, p = row_shifts(rate, rate_ref[t, PREV + v : PREV + v + 1, :], rate_ref[t, NEXT + v : NEXT + v + 1, :])
            e, w = east_west(rate)
            n, p, e, w = scale_n * n, scale_p * p, scale_e * e, scale_w * w
            across.append(n - p)
            along.append(e - w)
            smooth.append(centre * rate + damp * ((n + p) + (e + w)))
        for u in range(VARS):
            rows = pl.ds(u * SLAB, SLAB)
            total = sent_ref[t, rows, :] + smooth[u]
            for v in range(VARS):
                total = total - scale_row[u][v] * across[v] - scale_cell[u][v] * along[v]
            sent_ref[t, rows, :] = total
        return carry

    def sent_copy(g):
        part = pl.ds(pl.multiple_of(g * GROUP, GROUP), GROUP)
        return pltpu.make_async_copy(sent_ref.at[part], out_ref.at[part], written.at[g])

    def group(g, carry):
        for k in range(GROUP):
            instance(g * GROUP + k, 0)
        sent_copy(g).start()
        return carry

    lax.fori_loop(0, INST // GROUP, group, 0)
    for g in range(INST // GROUP):
        sent_copy(g).wait()


def face_kernel(live_ref, weights_ref, got_ref, half_ref, step_ref, out_ref):
    first = lax.axis_index("blk") * BLOCKS
    me = lax.axis_index("inst")
    total = jnp.zeros((FACES * VARS, CELLS), jnp.float32)
    for s in range(INST):
        total = total + weights_ref[me, s] * got_ref[s, FACE : FACE + FACES * VARS, :]
    out_ref[FACES * VARS :, :] = total
    for b in range(BLOCKS):
        for side in range(2):
            row = (live_ref[first + b] - 1) if side else 0
            scale = 0.5 * step_ref[b, pl.ds(row, 1), :]
            at = (2 * b + side) * VARS
            out_ref[at : at + VARS, :] = half_ref[at : at + VARS, :] - scale * total[at : at + VARS, :]


def ghost_kernel(live_ref, partner_ref, row_ref, visc_ref, step_ref, gathered_ref, spatial_in, spatial_ref):
    del spatial_in
    first = lax.axis_index("blk") * BLOCKS
    for b in range(BLOCKS):
        for side in range(2):
            place, local = ghost_place(partner_ref, 2 * b + side, ORDER2)
            row = (live_ref[first + b] - 1) if side else 0
            sign = 0.5 if side else -0.5
            rows = pl.ds(row, 1)
            step = step_ref[b, rows, :]
            damp = 0.25 + visc_ref[b, rows, :]
            ghost = [
                gathered_ref[place, pl.ds(local * VARS + v, 1), :]
                - 0.5 * step * gathered_ref[place, pl.ds((FACES + local) * VARS + v, 1), :]
                for v in range(VARS)
            ]
            for u in range(VARS):
                total = -damp * ghost[u]
                for v in range(VARS):
                    total = total + (sign * row_ref[u, v]) * ghost[v]
                spatial_ref[u, b, rows, :] = spatial_ref[u, b, rows, :] + total


def final_kernel(state_ref, step_ref, mask_ref, spatial_ref, got_ref, new_out, residual_out, new_ref, residual_ref, written):
    span = ROWS // 2

    def out_copies(k):
        b, rows = k // 2, pl.ds(pl.multiple_of((k % 2) * span, span), span)
        return [
            pltpu.make_async_copy(held.at[:, b, rows], out.at[0, :, b, rows], written.at[2 * k + n])
            for n, (held, out) in enumerate(((new_ref, new_out), (residual_ref, residual_out)))
        ]

    def part(k, carry):
        b = k // 2
        for j in range(PER_BLOCK // 2):
            slab = k * (PER_BLOCK // 2) + j
            rows = pl.ds(pl.multiple_of((k % 2) * span + j * SLAB, SLAB), SLAB)
            step, mask = step_ref[b, rows, :], mask_ref[b, rows, :]
            for v in range(VARS):
                total = mask * got_ref[slab, v * SLAB : (v + 1) * SLAB, :] + spatial_ref[v, b, rows, :]
                residual_ref[v, b, rows, :] = total
                new_ref[v, b, rows, :] = state_ref[0, v, b, rows, :] - step * total
        for copy in out_copies(k):
            copy.start()
        return carry

    lax.fori_loop(0, 2 * BLOCKS, part, 0)
    for k in range(2 * BLOCKS):
        for copy in out_copies(k):
            copy.wait()


def call(body, outs, in_specs, scratch=(), name=None, out_specs=None, limit=32, aliases=None):
    return pl.pallas_call(
        body,
        out_shape=[jax.ShapeDtypeStruct(shape, jnp.float32) for shape in outs],
        in_specs=in_specs,
        out_specs=out_specs or [VMEM] * len(outs),
        scratch_shapes=list(scratch),
        compiler_params=pltpu.CompilerParams(vmem_limit_bytes=limit * 1024 * 1024),
        input_output_aliases=aliases or {},
        name=name,
    )


def gathered_over_blocks(value, order):
    def moved(array, y=0, x=0, core=0):
        pairs = []
        for to in range(16):
            source = ((to // 8 + y) % 2) * 8 + (((to // 2) % 4 + x) % 4) * 2 + (to + core) % 2
            pairs.append((source, to))
        return lax.ppermute(array, "blk", pairs)

    value = value[None]
    for stage in order:
        steps = itertools.product(*(range(SIZES[axis]) for axis in stage))
        moves = [moved(value, **dict(zip(stage, step))) for step in list(steps)[1:]]
        value = jnp.concatenate([value] + moves)
    return value


def per_device(state, row_jacobian, cell_jacobian, viscosity, local_step, live_rows, partner):
    whole = state.shape
    chunks, faces = call(
        pack_kernel, [(INST, SENT // SLAB, SLAB, CELLS), (FACES * VARS, CELLS)], [HBM, HBM],
        [LIVE, pltpu.SemaphoreType.DMA((INST,)), pltpu.SemaphoreType.DMA((1,))], name="pack", limit=60
    )(live_rows, state)
    slabs = lax.all_to_all(chunks, "inst", 0, 0, tiled=True).reshape(INST, SENT, CELLS)
    ghosts = gathered_over_blocks(faces, ORDER)
    spatial, half_faces, mask = call(
        spatial_kernel,
        [(VARS, BLOCKS, ROWS, CELLS), (FACES * VARS, CELLS), (BLOCKS, ROWS, CELLS)],
        [SMEM, SMEM, SMEM, SMEM, VMEM, VMEM, VMEM, VMEM],
        [pltpu.VMEM((VARS, BLOCKS, ROWS, CELLS), jnp.float32)],
        name="spatial",
    )(live_rows, partner, row_jacobian, cell_jacobian, state, viscosity, local_step, ghosts)
    slabs, spatial = lax.optimization_barrier((slabs, spatial))
    (sent,) = call(
        slab_kernel, [(INST, MAIN, CELLS)], [HBM, HBM, HBM, VMEM, VMEM, VMEM],
        [
            pltpu.VMEM((INST, MAIN, CELLS), jnp.float32),
            pltpu.VMEM((INST, 96, CELLS), jnp.float32),
            LIVE,
            JACOBIAN,
            JACOBIAN,
            pltpu.SemaphoreType.DMA((3,)),
            pltpu.SemaphoreType.DMA((INST // GROUP,)),
        ],
        name="slab", out_specs=[HBM],
    )(live_rows, row_jacobian, cell_jacobian, slabs, viscosity, local_step)
    back = lax.all_to_all(sent, "inst", 0, 0, tiled=True)
    weights = jnp.array([[spectral(t - s) for s in range(INST)] for t in range(INST)], jnp.float32)
    (faces2,) = call(
        face_kernel, [(2 * FACES * VARS, CELLS)], [SMEM, SMEM, VMEM, VMEM, VMEM], name="faces"
    )(live_rows, weights, slabs, half_faces, local_step)
    ghosts2 = gathered_over_blocks(faces2, ORDER2)
    (spatial,) = call(
        ghost_kernel, [(VARS, BLOCKS, ROWS, CELLS)], [SMEM, SMEM, SMEM] + [VMEM] * 4, name="ghosts", aliases={6: 0}
    )(live_rows, partner, row_jacobian, viscosity, local_step, ghosts2, spatial)
    new_state, residual = call(
        final_kernel, [whole, whole], [VMEM] * 5,
        [pltpu.VMEM((VARS, BLOCKS, ROWS, CELLS), jnp.float32)] * 2 + [pltpu.SemaphoreType.DMA((4 * BLOCKS,))],
        name="final", out_specs=[HBM] * 2,
    )(state, local_step, mask, spatial, back)
    return new_state, residual


def solution(mesh):
    return jax.shard_map(
        per_device,
        mesh=mesh,
        in_specs=(
            P("inst", None, "blk", None, None),
            P(),
            P(),
            P("blk", None, None),
            P("blk", None, None),
            P(),
            P(),
        ),
        out_specs=(P("inst", None, "blk", None, None), P("inst", None, "blk", None, None)),
        check_vma=False,
    )
```

```python
import itertools
import math

import jax
import jax.numpy as jnp
from jax import lax
from jax.experimental import pallas as pl
from jax.experimental.pallas import tpu as pltpu
from jax.sharding import PartitionSpec as P

VARS, BLOCKS, ROWS, CELLS, INST = 5, 2, 128, 128, 16
SLAB = 16
PER_BLOCK = ROWS // SLAB
MAIN = VARS * SLAB
PREV, NEXT, FACE = MAIN, MAIN + VARS, MAIN + 2 * VARS
SENT = 112
FACES = 2 * BLOCKS
VMEM = pl.BlockSpec(memory_space=pltpu.VMEM)
SMEM = pl.BlockSpec(memory_space=pltpu.SMEM)
HBM = pl.BlockSpec(memory_space=pltpu.HBM)

SIZES = {"y": 2, "x": 4, "core": 2}
ORDER = (("y", "core",), ("x",),)
ORDER2 = (("y", "core",), ("x",),)
LIVE = pltpu.SMEM((32,), jnp.int32)
JACOBIAN = pltpu.SMEM((VARS, VARS), jnp.float32)


def spectral(m):
    m = m % INST
    if m in (0, INST // 2):
        return 0.0
    return 0.5 * (-1.0) ** m * math.cos(math.pi * m / INST) / math.sin(math.pi * m / INST)


HALF = INST // 2
GROUP = 8
EVEN = [0.5 * (spectral(m) + spectral(m + HALF)) for m in range(HALF)]
ODD = [0.5 * (spectral(m) - spectral(m + HALF)) for m in range(HALF)]


def weighted(terms):
    total = None
    for weight, value in terms:
        term = weight * value
        total = term if total is None else total + term
    return total


def apply_even(p):
    return [
        weighted([(EVEN[m], p[(t - m) % HALF] - p[(t + m) % HALF]) for m in range(1, HALF // 2)])
        for t in range(HALF)
    ]


def apply_odd(q):
    def at(index):
        index %= INST
        return q[index] if index < HALF else -q[index - HALF]

    def pair(t, m):
        low, high = (t - m) % INST, (t + m) % INST
        first = q[low % HALF] if low < HALF else None
        second = q[high % HALF] if high < HALF else None
        a, b = q[low % HALF], q[high % HALF]
        if first is not None and second is not None:
            return a - b, 1.0
        if first is None and second is not None:
            return a + b, -1.0
        if first is not None:
            return a + b, 1.0
        return a - b, -1.0

    result = []
    for t in range(HALF):
        terms = []
        for m in range(1, HALF // 2):
            value, sign = pair(t, m)
            terms.append((sign * ODD[m], value))
        last = (t - HALF // 2) % INST
        terms.append((ODD[HALF // 2] if last < HALF else -ODD[HALF // 2], q[last % HALF]))
        result.append(weighted(terms))
    return result


def row_shifts(tile, before, after):
    rows = tile.shape[0]
    row = lax.broadcasted_iota(jnp.int32, tile.shape, 0)
    following = jnp.where(row == rows - 1, after, pltpu.roll(tile, rows - 1, 0))
    previous = jnp.where(row == 0, before, pltpu.roll(tile, 1, 0))
    return following, previous


def east_west(tile):
    return pltpu.roll(tile, CELLS - 1, 1), pltpu.roll(tile, 1, 1)


def fetched(sources, held, ready):
    copies = [pltpu.make_async_copy(a, b, ready.at[k]) for k, (a, b) in enumerate(zip(sources, held))]
    for copy in copies:
        copy.start()
    return copies


def pack_kernel(live_in, state_ref, chunks_ref, faces_ref, held_ref, live_ref, arrived, ready):
    first = lax.axis_index("blk") * BLOCKS
    scalars = fetched([live_in], [live_ref], ready)
    places = [(v, b) for v in range(VARS) for b in range(BLOCKS)]
    copies = [
        pltpu.make_async_copy(state_ref.at[0, v, b], held_ref.at[v, b], arrived.at[k])
        for k, (v, b) in enumerate(places)
    ]
    for copy in copies:
        copy.start()
    for (v, b), copy in zip(places, copies):
        copy.wait()
        for j in range(PER_BLOCK):
            chunks_ref[b * PER_BLOCK + j, v] = held_ref[v, b, j * SLAB : (j + 1) * SLAB, :]
    for copy in scalars:
        copy.wait()

    def row_of(v, b, row):
        return held_ref[v, b, pl.ds(row, 1), :]

    for b in range(BLOCKS):
        last = live_ref[first + b] - 1
        for v in range(VARS):
            low, high = (2 * b) * VARS + v, (2 * b + 1) * VARS + v
            faces_ref[low : low + 1, :] = row_of(v, b, 0)
            faces_ref[high : high + 1, :] = row_of(v, b, last)
    faces = faces_ref[...]
    chunks_ref[0, VARS, 2 * VARS :, :] = faces[: SLAB - 2 * VARS, :]
    chunks_ref[0, VARS + 1, : FACES * VARS + 2 * VARS - SLAB, :] = faces[SLAB - 2 * VARS :, :]
    chunks_ref[0, VARS + 1, FACES * VARS + 2 * VARS - SLAB :, :] = jnp.zeros((SENT - FACE - FACES * VARS, CELLS), jnp.float32)
    chunks_ref[0, VARS, 0 : 2 * VARS, :] = jnp.zeros((2 * VARS, CELLS), jnp.float32)
    extra = chunks_ref[0, VARS : VARS + 2, :, :]
    for i in range(1, INST):
        chunks_ref[i, VARS : VARS + 2, :, :] = extra
    for i in range(INST):
        b, j = i // PER_BLOCK, i % PER_BLOCK
        for v in range(VARS):
            if j > 0:
                chunks_ref[i, VARS, v : v + 1, :] = row_of(v, b, j * SLAB - 1)
            if j < PER_BLOCK - 1:
                chunks_ref[i, VARS, VARS + v : VARS + v + 1, :] = row_of(v, b, (j + 1) * SLAB)


def ghost_place(partner_ref, face, order):
    me = lax.axis_index("blk")
    other = partner_ref[me * FACES + face]
    device, local = other // FACES, other % FACES
    away = {
        "core": (device % 2 + me % 2) % 2,
        "x": ((device // 2) % 4 - (me // 2) % 4 + 4) % 4,
        "y": (device // 8 + me // 8) % 2,
    }
    place = 0
    for stage in reversed(order):
        for axis in stage:
            place = place * SIZES[axis] + away[axis]
    return place, local


def spatial_kernel(live_ref, partner_ref, row_ref, cell_ref, state_ref, visc_ref, step_ref, gathered_ref,
                   spatial_ref, faces_ref, mask_ref, half_ref):
    first = lax.axis_index("blk") * BLOCKS

    def stencil(tiles, befores, afters, mask_n, mask_p, damp):
        across, along, smooth = [], [], []
        for v in range(VARS):
            n, p = row_shifts(tiles[v], befores[v], afters[v])
            n, p = n * mask_n, p * mask_p
            e, w = east_west(tiles[v])
            across.append(n - p)
            along.append(e - w)
            smooth.append((n + p) + (e + w) - 4.0 * tiles[v])
        result = []
        for u in range(VARS):
            total = -damp * smooth[u]
            for v in range(VARS):
                total = total + (0.5 * row_ref[u, v]) * across[v] + (0.5 * cell_ref[u, v]) * along[v]
            result.append(total)
        return result

    def sweep(read, write, b, live):
        def step(j, carry):
            low = pl.multiple_of(j * SLAB, SLAB)
            before, after = jnp.maximum(low - 1, 0), jnp.minimum(low + SLAB, ROWS - 1)
            row = low + lax.broadcasted_iota(jnp.int32, (SLAB, CELLS), 0)
            mask_n = jnp.where(row + 1 < live, 1.0, 0.0)
            mask_p = jnp.where(row > 0, 1.0, 0.0)
            damp = 0.25 + visc_ref[b, pl.ds(low, SLAB), :]
            tiles = [read(v, b, pl.ds(low, SLAB)) for v in range(VARS)]
            befores = [read(v, b, pl.ds(before, 1)) for v in range(VARS)]
            afters = [read(v, b, pl.ds(after, 1)) for v in range(VARS)]
            result = stencil(tiles, befores, afters, mask_n, mask_p, damp)
            write(b, low, tiles, result)
            return carry

        lax.fori_loop(0, PER_BLOCK, step, 0)

    def read_state(v, b, rows):
        return state_ref[0, v, b, rows, :]

    def read_half(v, b, rows):
        return half_ref[v, b, rows, :]

    def write_half(b, low, tiles, result):
        scale = 0.5 * step_ref[b, pl.ds(low, SLAB), :]
        for v in range(VARS):
            half_ref[v, b, pl.ds(low, SLAB), :] = tiles[v] - scale * result[v]

    def write_spatial(b, low, tiles, result):
        row = low + lax.broadcasted_iota(jnp.int32, (SLAB, CELLS), 0)
        inside = row < live_ref[first + b]
        mask_ref[b, pl.ds(low, SLAB), :] = jnp.where(inside, 1.0, 0.0)
        for v in range(VARS):
            spatial_ref[v, b, pl.ds(low, SLAB), :] = jnp.where(inside, result[v], 0.0)

    for b in range(BLOCKS):
        live = live_ref[first + b]
        sweep(read_state, write_half, b, live)
        for side in range(2):
            place, local = ghost_place(partner_ref, 2 * b + side, ORDER)
            row = (live - 1) if side else 0
            sign = 0.5 if side else -0.5
            rows = pl.ds(row, 1)
            ghost = [gathered_ref[place, pl.ds(local * VARS + v, 1), :] for v in range(VARS)]
            damp = 0.25 + visc_ref[b, rows, :]
            scale = 0.5 * step_ref[b, rows, :]
            for u in range(VARS):
                total = -damp * ghost[u]
                for v in range(VARS):
                    total = total + (sign * row_ref[u, v]) * ghost[v]
                half_ref[u, b, rows, :] = half_ref[u, b, rows, :] - scale * total
        for side in range(2):
            row = (live - 1) if side else 0
            for v in range(VARS):
                faces_ref[pl.ds((2 * b + side) * VARS + v, 1), :] = half_ref[v, b, pl.ds(row, 1), :]
        sweep(read_half, write_spatial, b, live)


def slab_kernel(live_in, row_in, cell_in, got_ref, visc_ref, step_ref, out_ref, sent_ref, rate_ref, live_ref, row_ref, cell_ref, ready, written):
    scalars = fetched([live_in, row_in, cell_in], [live_ref, row_ref, cell_ref], ready)
    i = lax.axis_index("inst")
    b, j = i // PER_BLOCK, i % PER_BLOCK
    low = pl.multiple_of(j * SLAB, SLAB)
    step = step_ref[b, pl.ds(low, SLAB), :]

    def times(rows, with_second):
        values = [got_ref[t, rows, :] for t in range(INST)]
        p = [values[t] + values[t + HALF] for t in range(HALF)]
        q = [values[t] - values[t + HALF] for t in range(HALF)]
        p, q = apply_even(p), apply_odd(q)
        for t in range(HALF):
            rate_ref[t, rows, :] = p[t] + q[t]
            rate_ref[t + HALF, rows, :] = p[t] - q[t]
        if with_second is not None:
            p, q = apply_even(p), apply_odd(q)
            for t in range(HALF):
                sent_ref[t, rows, :] = with_second * (p[t] + q[t])
                sent_ref[t + HALF, rows, :] = with_second * (p[t] - q[t])

    half_step = [-step[0:8, :], -step[8:16, :]]
    for v in range(VARS):
        for k in range(2):
            at = v * SLAB + 8 * k
            times(slice(at, at + 8), half_step[k])
    times(slice(MAIN, MAIN + 8), None)
    times(slice(MAIN + 8, MAIN + 16), None)
    for copy in scalars:
        copy.wait()
    live = live_ref[lax.axis_index("blk") * BLOCKS + b]
    step_before = step_ref[b, pl.ds(jnp.maximum(low - 1, 0), 1), :]
    step_after = step_ref[b, pl.ds(jnp.minimum(low + SLAB, ROWS - 1), 1), :]
    row = low + lax.broadcasted_iota(jnp.int32, (SLAB, CELLS), 0)
    step_n, step_p = row_shifts(step, step_before, step_after)
    step_e, step_w = east_west(step)
    scale_n = jnp.where(row + 1 < live, step + step_n, 0.0)
    scale_p = jnp.where(row > 0, step + step_p, 0.0)
    scale_e, scale_w = step + step_e, step + step_w
    damp = 0.5 * (0.25 + visc_ref[b, pl.ds(low, SLAB), :])
    centre = 1.0 - 8.0 * step * damp

    def spread(coefficients):
        return [[jnp.full((SLAB, CELLS), 0.25 * coefficients[u, v]) for v in range(VARS)] for u in range(VARS)]

    scale_row, scale_cell = spread(row_ref), spread(cell_ref)

    def instance(t, carry):
        across, along, smooth = [], [], []
        for v in range(VARS):
            rate = rate_ref[t, pl.ds(v * SLAB, SLAB), :]
            n, p = row_shifts(rate, rate_ref[t, PREV + v : PREV + v + 1, :], rate_ref[t, NEXT + v : NEXT + v + 1, :])
            e, w = east_west(rate)
            n, p, e, w = scale_n * n, scale_p * p, scale_e * e, scale_w * w
            across.append(n - p)
            along.append(e - w)
            smooth.append(centre * rate + damp * ((n + p) + (e + w)))
        for u in range(VARS):
            rows = pl.ds(u * SLAB, SLAB)
            total = sent_ref[t, rows, :] + smooth[u]
            for v in range(VARS):
                total = total - scale_row[u][v] * across[v] - scale_cell[u][v] * along[v]
            sent_ref[t, rows, :] = total
        return carry

    def sent_copy(g):
        part = pl.ds(pl.multiple_of(g * GROUP, GROUP), GROUP)
        return pltpu.make_async_copy(sent_ref.at[part], out_ref.at[part], written.at[g])

    def group(g, carry):
        for k in range(GROUP):
            instance(g * GROUP + k, 0)
        sent_copy(g).start()
        return carry

    lax.fori_loop(0, INST // GROUP, group, 0)
    for g in range(INST // GROUP):
        sent_copy(g).wait()


def face_kernel(live_ref, weights_ref, got_ref, half_ref, step_ref, out_ref):
    first = lax.axis_index("blk") * BLOCKS
    me = lax.axis_index("inst")
    total = jnp.zeros((FACES * VARS, CELLS), jnp.float32)
    for s in range(INST):
        total = total + weights_ref[me, s] * got_ref[s, FACE : FACE + FACES * VARS, :]
    out_ref[FACES * VARS :, :] = total
    for b in range(BLOCKS):
        for side in range(2):
            row = (live_ref[first + b] - 1) if side else 0
            scale = 0.5 * step_ref[b, pl.ds(row, 1), :]
            at = (2 * b + side) * VARS
            out_ref[at : at + VARS, :] = half_ref[at : at + VARS, :] - scale * total[at : at + VARS, :]


def ghost_kernel(live_ref, partner_ref, row_ref, visc_ref, step_ref, gathered_ref, spatial_in, spatial_ref):
    del spatial_in
    first = lax.axis_index("blk") * BLOCKS
    for b in range(BLOCKS):
        for side in range(2):
            place, local = ghost_place(partner_ref, 2 * b + side, ORDER2)
            row = (live_ref[first + b] - 1) if side else 0
            sign = 0.5 if side else -0.5
            rows = pl.ds(row, 1)
            step = step_ref[b, rows, :]
            damp = 0.25 + visc_ref[b, rows, :]
            ghost = [
                gathered_ref[place, pl.ds(local * VARS + v, 1), :]
                - 0.5 * step * gathered_ref[place, pl.ds((FACES + local) * VARS + v, 1), :]
                for v in range(VARS)
            ]
            for u in range(VARS):
                total = -damp * ghost[u]
                for v in range(VARS):
                    total = total + (sign * row_ref[u, v]) * ghost[v]
                spatial_ref[u, b, rows, :] = spatial_ref[u, b, rows, :] + total


def final_kernel(state_ref, step_ref, mask_ref, spatial_ref, got_ref, new_out, residual_out, new_ref, residual_ref, written):
    span = ROWS // 2

    def out_copies(k):
        b, rows = k // 2, pl.ds(pl.multiple_of((k % 2) * span, span), span)
        return [
            pltpu.make_async_copy(held.at[:, b, rows], out.at[0, :, b, rows], written.at[2 * k + n])
            for n, (held, out) in enumerate(((new_ref, new_out), (residual_ref, residual_out)))
        ]

    def part(k, carry):
        b = k // 2
        for j in range(PER_BLOCK // 2):
            slab = k * (PER_BLOCK // 2) + j
            rows = pl.ds(pl.multiple_of((k % 2) * span + j * SLAB, SLAB), SLAB)
            step, mask = step_ref[b, rows, :], mask_ref[b, rows, :]
            for v in range(VARS):
                total = mask * got_ref[slab, v * SLAB : (v + 1) * SLAB, :] + spatial_ref[v, b, rows, :]
                residual_ref[v, b, rows, :] = total
                new_ref[v, b, rows, :] = state_ref[0, v, b, rows, :] - step * total
        for copy in out_copies(k):
            copy.start()
        return carry

    lax.fori_loop(0, 2 * BLOCKS, part, 0)
    for k in range(2 * BLOCKS):
        for copy in out_copies(k):
            copy.wait()


def call(body, outs, in_specs, scratch=(), name=None, out_specs=None, limit=32, aliases=None):
    return pl.pallas_call(
        body,
        out_shape=[jax.ShapeDtypeStruct(shape, jnp.float32) for shape in outs],
        in_specs=in_specs,
        out_specs=out_specs or [VMEM] * len(outs),
        scratch_shapes=list(scratch),
        compiler_params=pltpu.CompilerParams(vmem_limit_bytes=limit * 1024 * 1024),
        input_output_aliases=aliases or {},
        name=name,
    )


def gathered_over_blocks(value, order):
    def moved(array, y=0, x=0, core=0):
        pairs = []
        for to in range(16):
            source = ((to // 8 + y) % 2) * 8 + (((to // 2) % 4 + x) % 4) * 2 + (to + core) % 2
            pairs.append((source, to))
        return lax.ppermute(array, "blk", pairs)

    value = value[None]
    for stage in order:
        steps = itertools.product(*(range(SIZES[axis]) for axis in stage))
        moves = [moved(value, **dict(zip(stage, step))) for step in list(steps)[1:]]
        value = jnp.concatenate([value] + moves)
    return value


def per_device(state, row_jacobian, cell_jacobian, viscosity, local_step, live_rows, partner):
    whole = state.shape
    chunks, faces = call(
        pack_kernel, [(INST, SENT // SLAB, SLAB, CELLS), (FACES * VARS, CELLS)], [HBM, HBM],
        [
            pltpu.VMEM((VARS, BLOCKS, ROWS, CELLS), jnp.float32),
            LIVE,
            pltpu.SemaphoreType.DMA((VARS * BLOCKS,)),
            pltpu.SemaphoreType.DMA((1,)),
        ],
        name="pack", limit=60
    )(live_rows, state)
    slabs = lax.all_to_all(chunks, "inst", 0, 0, tiled=True).reshape(INST, SENT, CELLS)
    ghosts = gathered_over_blocks(faces, ORDER)
    spatial, half_faces, mask = call(
        spatial_kernel,
        [(VARS, BLOCKS, ROWS, CELLS), (FACES * VARS, CELLS), (BLOCKS, ROWS, CELLS)],
        [SMEM, SMEM, SMEM, SMEM, VMEM, VMEM, VMEM, VMEM],
        [pltpu.VMEM((VARS, BLOCKS, ROWS, CELLS), jnp.float32)],
        name="spatial",
    )(live_rows, partner, row_jacobian, cell_jacobian, state, viscosity, local_step, ghosts)
    slabs, spatial = lax.optimization_barrier((slabs, spatial))
    (sent,) = call(
        slab_kernel, [(INST, MAIN, CELLS)], [HBM, HBM, HBM, VMEM, VMEM, VMEM],
        [
            pltpu.VMEM((INST, MAIN, CELLS), jnp.float32),
            pltpu.VMEM((INST, 96, CELLS), jnp.float32),
            LIVE,
            JACOBIAN,
            JACOBIAN,
            pltpu.SemaphoreType.DMA((3,)),
            pltpu.SemaphoreType.DMA((INST // GROUP,)),
        ],
        name="slab", out_specs=[HBM],
    )(live_rows, row_jacobian, cell_jacobian, slabs, viscosity, local_step)
    back = lax.all_to_all(sent, "inst", 0, 0, tiled=True)
    weights = jnp.array([[spectral(t - s) for s in range(INST)] for t in range(INST)], jnp.float32)
    (faces2,) = call(
        face_kernel, [(2 * FACES * VARS, CELLS)], [SMEM, SMEM, VMEM, VMEM, VMEM], name="faces"
    )(live_rows, weights, slabs, half_faces, local_step)
    ghosts2 = gathered_over_blocks(faces2, ORDER2)
    (spatial,) = call(
        ghost_kernel, [(VARS, BLOCKS, ROWS, CELLS)], [SMEM, SMEM, SMEM] + [VMEM] * 4, name="ghosts", aliases={6: 0}
    )(live_rows, partner, row_jacobian, viscosity, local_step, ghosts2, spatial)
    new_state, residual = call(
        final_kernel, [whole, whole], [VMEM] * 5,
        [pltpu.VMEM((VARS, BLOCKS, ROWS, CELLS), jnp.float32)] * 2 + [pltpu.SemaphoreType.DMA((4 * BLOCKS,))],
        name="final", out_specs=[HBM] * 2,
    )(state, local_step, mask, spatial, back)
    return new_state, residual


def solution(mesh):
    return jax.shard_map(
        per_device,
        mesh=mesh,
        in_specs=(
            P("inst", None, "blk", None, None),
            P(),
            P(),
            P("blk", None, None),
            P("blk", None, None),
            P(),
            P(),
        ),
        out_specs=(P("inst", None, "blk", None, None), P("inst", None, "blk", None, None)),
        check_vma=False,
    )
```

```python
import itertools
import math

import jax
import jax.numpy as jnp
import numpy as np
from jax import lax
from jax.experimental import pallas as pl
from jax.experimental.pallas import tpu as pltpu
from jax.sharding import PartitionSpec as P

VARS, BLOCKS, ROWS, CELLS, INST = 5, 2, 128, 128, 16
SLAB = 16
PER_BLOCK = ROWS // SLAB
MAIN = VARS * SLAB
PREV, NEXT, FACE = MAIN, MAIN + VARS, MAIN + 2 * VARS
SENT = 112
FACES = 2 * BLOCKS
VMEM = pl.BlockSpec(memory_space=pltpu.VMEM)
SMEM = pl.BlockSpec(memory_space=pltpu.SMEM)
HBM = pl.BlockSpec(memory_space=pltpu.HBM)

SIZES = {"y": 2, "x": 4, "core": 2}
ORDER = (("y", "core",), ("x",),)
ORDER2 = (("y", "core",), ("x",),)
LIVE = pltpu.SMEM((32,), jnp.int32)
JACOBIAN = pltpu.SMEM((VARS, VARS), jnp.float32)


def spectral(m):
    m = m % INST
    if m in (0, INST // 2):
        return 0.0
    return 0.5 * (-1.0) ** m * math.cos(math.pi * m / INST) / math.sin(math.pi * m / INST)


HALF = INST // 2
GROUP = 8
EVEN = [0.5 * (spectral(m) + spectral(m + HALF)) for m in range(HALF)]
ODD = [0.5 * (spectral(m) - spectral(m + HALF)) for m in range(HALF)]


def weighted(terms):
    total = None
    for weight, value in terms:
        term = weight * value
        total = term if total is None else total + term
    return total


def apply_even(p):
    return [
        weighted([(EVEN[m], p[(t - m) % HALF] - p[(t + m) % HALF]) for m in range(1, HALF // 2)])
        for t in range(HALF)
    ]


def apply_odd(q):
    def at(index):
        index %= INST
        return q[index] if index < HALF else -q[index - HALF]

    def pair(t, m):
        low, high = (t - m) % INST, (t + m) % INST
        first = q[low % HALF] if low < HALF else None
        second = q[high % HALF] if high < HALF else None
        a, b = q[low % HALF], q[high % HALF]
        if first is not None and second is not None:
            return a - b, 1.0
        if first is None and second is not None:
            return a + b, -1.0
        if first is not None:
            return a + b, 1.0
        return a - b, -1.0

    result = []
    for t in range(HALF):
        terms = []
        for m in range(1, HALF // 2):
            value, sign = pair(t, m)
            terms.append((sign * ODD[m], value))
        last = (t - HALF // 2) % INST
        terms.append((ODD[HALF // 2] if last < HALF else -ODD[HALF // 2], q[last % HALF]))
        result.append(weighted(terms))
    return result


def row_shifts(tile, before, after):
    rows = tile.shape[0]
    row = lax.broadcasted_iota(jnp.int32, tile.shape, 0)
    following = jnp.where(row == rows - 1, after, pltpu.roll(tile, rows - 1, 0))
    previous = jnp.where(row == 0, before, pltpu.roll(tile, 1, 0))
    return following, previous


def east_west(tile):
    return pltpu.roll(tile, CELLS - 1, 1), pltpu.roll(tile, 1, 1)


def fetched(sources, held, ready):
    copies = [pltpu.make_async_copy(a, b, ready.at[k]) for k, (a, b) in enumerate(zip(sources, held))]
    for copy in copies:
        copy.start()
    return copies


def pack_kernel(live_in, state_ref, chunks_ref, faces_ref, held_ref, live_ref, arrived, ready):
    first = lax.axis_index("blk") * BLOCKS
    scalars = fetched([live_in], [live_ref], ready)
    places = [(v, b) for v in range(VARS) for b in range(BLOCKS)]
    copies = [
        pltpu.make_async_copy(state_ref.at[0, v, b], held_ref.at[v, b], arrived.at[k])
        for k, (v, b) in enumerate(places)
    ]
    for copy in copies:
        copy.start()
    for (v, b), copy in zip(places, copies):
        copy.wait()
        for j in range(PER_BLOCK):
            chunks_ref[b * PER_BLOCK + j, v] = held_ref[v, b, j * SLAB : (j + 1) * SLAB, :]
    for copy in scalars:
        copy.wait()

    def row_of(v, b, row):
        return held_ref[v, b, pl.ds(row, 1), :]

    for b in range(BLOCKS):
        last = live_ref[first + b] - 1
        for v in range(VARS):
            low, high = (2 * b) * VARS + v, (2 * b + 1) * VARS + v
            faces_ref[low : low + 1, :] = row_of(v, b, 0)
            faces_ref[high : high + 1, :] = row_of(v, b, last)
    faces = faces_ref[...]
    chunks_ref[0, VARS, 2 * VARS :, :] = faces[: SLAB - 2 * VARS, :]
    chunks_ref[0, VARS + 1, : FACES * VARS + 2 * VARS - SLAB, :] = faces[SLAB - 2 * VARS :, :]
    chunks_ref[0, VARS + 1, FACES * VARS + 2 * VARS - SLAB :, :] = jnp.zeros((SENT - FACE - FACES * VARS, CELLS), jnp.float32)
    chunks_ref[0, VARS, 0 : 2 * VARS, :] = jnp.zeros((2 * VARS, CELLS), jnp.float32)
    extra = chunks_ref[0, VARS : VARS + 2, :, :]
    for i in range(1, INST):
        chunks_ref[i, VARS : VARS + 2, :, :] = extra
    for i in range(INST):
        b, j = i // PER_BLOCK, i % PER_BLOCK
        for v in range(VARS):
            if j > 0:
                chunks_ref[i, VARS, v : v + 1, :] = row_of(v, b, j * SLAB - 1)
            if j < PER_BLOCK - 1:
                chunks_ref[i, VARS, VARS + v : VARS + v + 1, :] = row_of(v, b, (j + 1) * SLAB)


def ghost_place(partner_ref, face, order):
    me = lax.axis_index("blk")
    other = partner_ref[me * FACES + face]
    device, local = other // FACES, other % FACES
    away = {
        "core": (device % 2 + me % 2) % 2,
        "x": ((device // 2) % 4 - (me // 2) % 4 + 4) % 4,
        "y": (device // 8 + me // 8) % 2,
    }
    place = 0
    for stage in reversed(order):
        for axis in stage:
            place = place * SIZES[axis] + away[axis]
    return place, local


def spatial_kernel(live_ref, partner_ref, row_ref, cell_ref, state_ref, visc_ref, step_ref, gathered_ref,
                   spatial_ref, faces_ref, mask_ref, half_ref):
    first = lax.axis_index("blk") * BLOCKS

    def stencil(tiles, befores, afters, mask_n, mask_p, damp):
        across, along, smooth = [], [], []
        for v in range(VARS):
            n, p = row_shifts(tiles[v], befores[v], afters[v])
            n, p = n * mask_n, p * mask_p
            e, w = east_west(tiles[v])
            across.append(n - p)
            along.append(e - w)
            smooth.append((n + p) + (e + w) - 4.0 * tiles[v])
        result = []
        for u in range(VARS):
            total = -damp * smooth[u]
            for v in range(VARS):
                total = total + (0.5 * row_ref[u, v]) * across[v] + (0.5 * cell_ref[u, v]) * along[v]
            result.append(total)
        return result

    def sweep(read, write, b, live):
        def step(j, carry):
            low = pl.multiple_of(j * SLAB, SLAB)
            before, after = jnp.maximum(low - 1, 0), jnp.minimum(low + SLAB, ROWS - 1)
            row = low + lax.broadcasted_iota(jnp.int32, (SLAB, CELLS), 0)
            mask_n = jnp.where(row + 1 < live, 1.0, 0.0)
            mask_p = jnp.where(row > 0, 1.0, 0.0)
            damp = 0.25 + visc_ref[b, pl.ds(low, SLAB), :]
            tiles = [read(v, b, pl.ds(low, SLAB)) for v in range(VARS)]
            befores = [read(v, b, pl.ds(before, 1)) for v in range(VARS)]
            afters = [read(v, b, pl.ds(after, 1)) for v in range(VARS)]
            result = stencil(tiles, befores, afters, mask_n, mask_p, damp)
            write(b, low, tiles, result)
            return carry

        lax.fori_loop(0, PER_BLOCK, step, 0)

    def read_state(v, b, rows):
        return state_ref[0, v, b, rows, :]

    def read_half(v, b, rows):
        return half_ref[v, b, rows, :]

    def write_half(b, low, tiles, result):
        scale = 0.5 * step_ref[b, pl.ds(low, SLAB), :]
        for v in range(VARS):
            half_ref[v, b, pl.ds(low, SLAB), :] = tiles[v] - scale * result[v]

    def write_spatial(b, low, tiles, result):
        row = low + lax.broadcasted_iota(jnp.int32, (SLAB, CELLS), 0)
        inside = row < live_ref[first + b]
        mask_ref[b, pl.ds(low, SLAB), :] = jnp.where(inside, 1.0, 0.0)
        for v in range(VARS):
            spatial_ref[v, b, pl.ds(low, SLAB), :] = jnp.where(inside, result[v], 0.0)

    for b in range(BLOCKS):
        live = live_ref[first + b]
        sweep(read_state, write_half, b, live)
        for side in range(2):
            place, local = ghost_place(partner_ref, 2 * b + side, ORDER)
            row = (live - 1) if side else 0
            sign = 0.5 if side else -0.5
            rows = pl.ds(row, 1)
            ghost = [gathered_ref[place, pl.ds(local * VARS + v, 1), :] for v in range(VARS)]
            damp = 0.25 + visc_ref[b, rows, :]
            scale = 0.5 * step_ref[b, rows, :]
            for u in range(VARS):
                total = -damp * ghost[u]
                for v in range(VARS):
                    total = total + (sign * row_ref[u, v]) * ghost[v]
                half_ref[u, b, rows, :] = half_ref[u, b, rows, :] - scale * total
        for side in range(2):
            row = (live - 1) if side else 0
            for v in range(VARS):
                faces_ref[pl.ds((2 * b + side) * VARS + v, 1), :] = half_ref[v, b, pl.ds(row, 1), :]
        sweep(read_half, write_spatial, b, live)


def slab_kernel(live_in, row_in, cell_in, got_ref, visc_ref, step_ref, out_ref, sent_ref, rate_ref, live_ref, row_ref, cell_ref, ready, written):
    scalars = fetched([live_in, row_in, cell_in], [live_ref, row_ref, cell_ref], ready)
    i = lax.axis_index("inst")
    b, j = i // PER_BLOCK, i % PER_BLOCK
    low = pl.multiple_of(j * SLAB, SLAB)
    step = step_ref[b, pl.ds(low, SLAB), :]

    def times(rows, with_second):
        values = [got_ref[t, rows, :] for t in range(INST)]
        p = [values[t] + values[t + HALF] for t in range(HALF)]
        q = [values[t] - values[t + HALF] for t in range(HALF)]
        p, q = apply_even(p), apply_odd(q)
        for t in range(HALF):
            rate_ref[t, rows, :] = p[t] + q[t]
            rate_ref[t + HALF, rows, :] = p[t] - q[t]
        if with_second is not None:
            p, q = apply_even(p), apply_odd(q)
            for t in range(HALF):
                sent_ref[t, rows, :] = with_second * (p[t] + q[t])
                sent_ref[t + HALF, rows, :] = with_second * (p[t] - q[t])

    half_step = [-step[0:8, :], -step[8:16, :]]
    for v in range(VARS):
        for k in range(2):
            at = v * SLAB + 8 * k
            times(slice(at, at + 8), half_step[k])
    times(slice(MAIN, MAIN + 8), None)
    times(slice(MAIN + 8, MAIN + 16), None)
    for copy in scalars:
        copy.wait()
    live = live_ref[lax.axis_index("blk") * BLOCKS + b]
    step_before = step_ref[b, pl.ds(jnp.maximum(low - 1, 0), 1), :]
    step_after = step_ref[b, pl.ds(jnp.minimum(low + SLAB, ROWS - 1), 1), :]
    row = low + lax.broadcasted_iota(jnp.int32, (SLAB, CELLS), 0)
    step_n, step_p = row_shifts(step, step_before, step_after)
    step_e, step_w = east_west(step)
    scale_n = jnp.where(row + 1 < live, step + step_n, 0.0)
    scale_p = jnp.where(row > 0, step + step_p, 0.0)
    scale_e, scale_w = step + step_e, step + step_w
    damp = 0.5 * (0.25 + visc_ref[b, pl.ds(low, SLAB), :])
    centre = 1.0 - 8.0 * step * damp

    def spread(coefficients):
        return [[jnp.full((SLAB, CELLS), 0.25 * coefficients[u, v]) for v in range(VARS)] for u in range(VARS)]

    scale_row, scale_cell = spread(row_ref), spread(cell_ref)

    def instance(t, carry):
        across, along, smooth = [], [], []
        for v in range(VARS):
            rate = rate_ref[t, pl.ds(v * SLAB, SLAB), :]
            n, p = row_shifts(rate, rate_ref[t, PREV + v : PREV + v + 1, :], rate_ref[t, NEXT + v : NEXT + v + 1, :])
            e, w = east_west(rate)
            n, p, e, w = scale_n * n, scale_p * p, scale_e * e, scale_w * w
            across.append(n - p)
            along.append(e - w)
            smooth.append(centre * rate + damp * ((n + p) + (e + w)))
        for u in range(VARS):
            rows = pl.ds(u * SLAB, SLAB)
            total = sent_ref[t, rows, :] + smooth[u]
            for v in range(VARS):
                total = total - scale_row[u][v] * across[v] - scale_cell[u][v] * along[v]
            sent_ref[t, rows, :] = total
        return carry

    def sent_copy(g):
        part = pl.ds(pl.multiple_of(g * GROUP, GROUP), GROUP)
        return pltpu.make_async_copy(sent_ref.at[part], out_ref.at[part], written.at[g])

    def group(g, carry):
        for k in range(GROUP):
            instance(g * GROUP + k, 0)
        sent_copy(g).start()
        return carry

    lax.fori_loop(0, INST // GROUP, group, 0)
    for g in range(INST // GROUP):
        sent_copy(g).wait()


def face_kernel(live_in, weights_ref, got_ref, half_ref, step_ref, out_ref, live_ref, ready):
    scalars = fetched([live_in], [live_ref], ready)
    first = lax.axis_index("blk") * BLOCKS
    me = lax.axis_index("inst")
    total = jnp.zeros((FACES * VARS, CELLS), jnp.float32)
    for s in range(INST):
        total = total + weights_ref[me, s : s + 1, :] * got_ref[s, FACE : FACE + FACES * VARS, :]
    out_ref[FACES * VARS :, :] = total
    for copy in scalars:
        copy.wait()
    for b in range(BLOCKS):
        for side in range(2):
            row = (live_ref[first + b] - 1) if side else 0
            scale = 0.5 * step_ref[b, pl.ds(row, 1), :]
            at = (2 * b + side) * VARS
            out_ref[at : at + VARS, :] = half_ref[at : at + VARS, :] - scale * total[at : at + VARS, :]


def ghost_kernel(live_ref, partner_ref, row_ref, visc_ref, step_ref, gathered_ref, spatial_in, spatial_ref):
    del spatial_in
    first = lax.axis_index("blk") * BLOCKS
    for b in range(BLOCKS):
        for side in range(2):
            place, local = ghost_place(partner_ref, 2 * b + side, ORDER2)
            row = (live_ref[first + b] - 1) if side else 0
            sign = 0.5 if side else -0.5
            rows = pl.ds(row, 1)
            step = step_ref[b, rows, :]
            damp = 0.25 + visc_ref[b, rows, :]
            ghost = [
                gathered_ref[place, pl.ds(local * VARS + v, 1), :]
                - 0.5 * step * gathered_ref[place, pl.ds((FACES + local) * VARS + v, 1), :]
                for v in range(VARS)
            ]
            for u in range(VARS):
                total = -damp * ghost[u]
                for v in range(VARS):
                    total = total + (sign * row_ref[u, v]) * ghost[v]
                spatial_ref[u, b, rows, :] = spatial_ref[u, b, rows, :] + total


def final_kernel(state_ref, step_ref, mask_ref, spatial_ref, got_ref, new_out, residual_out, new_ref, residual_ref, written):
    span = ROWS // 2

    def out_copies(k):
        b, rows = k // 2, pl.ds(pl.multiple_of((k % 2) * span, span), span)
        return [
            pltpu.make_async_copy(held.at[:, b, rows], out.at[0, :, b, rows], written.at[2 * k + n])
            for n, (held, out) in enumerate(((new_ref, new_out), (residual_ref, residual_out)))
        ]

    def part(k, carry):
        b = k // 2
        for j in range(PER_BLOCK // 2):
            slab = k * (PER_BLOCK // 2) + j
            rows = pl.ds(pl.multiple_of((k % 2) * span + j * SLAB, SLAB), SLAB)
            step, mask = step_ref[b, rows, :], mask_ref[b, rows, :]
            for v in range(VARS):
                total = mask * got_ref[slab, v * SLAB : (v + 1) * SLAB, :] + spatial_ref[v, b, rows, :]
                residual_ref[v, b, rows, :] = total
                new_ref[v, b, rows, :] = state_ref[0, v, b, rows, :] - step * total
        for copy in out_copies(k):
            copy.start()
        return carry

    lax.fori_loop(0, 2 * BLOCKS, part, 0)
    for k in range(2 * BLOCKS):
        for copy in out_copies(k):
            copy.wait()


def call(body, outs, in_specs, scratch=(), name=None, out_specs=None, limit=32, aliases=None):
    return pl.pallas_call(
        body,
        out_shape=[jax.ShapeDtypeStruct(shape, jnp.float32) for shape in outs],
        in_specs=in_specs,
        out_specs=out_specs or [VMEM] * len(outs),
        scratch_shapes=list(scratch),
        compiler_params=pltpu.CompilerParams(vmem_limit_bytes=limit * 1024 * 1024),
        input_output_aliases=aliases or {},
        name=name,
    )


def gathered_over_blocks(value, order):
    def moved(array, y=0, x=0, core=0):
        pairs = []
        for to in range(16):
            source = ((to // 8 + y) % 2) * 8 + (((to // 2) % 4 + x) % 4) * 2 + (to + core) % 2
            pairs.append((source, to))
        return lax.ppermute(array, "blk", pairs)

    value = value[None]
    for stage in order:
        steps = itertools.product(*(range(SIZES[axis]) for axis in stage))
        moves = [moved(value, **dict(zip(stage, step))) for step in list(steps)[1:]]
        value = jnp.concatenate([value] + moves)
    return value


def per_device(state, row_jacobian, cell_jacobian, viscosity, local_step, live_rows, partner):
    whole = state.shape
    chunks, faces = call(
        pack_kernel, [(INST, SENT // SLAB, SLAB, CELLS), (FACES * VARS, CELLS)], [HBM, HBM],
        [
            pltpu.VMEM((VARS, BLOCKS, ROWS, CELLS), jnp.float32),
            LIVE,
            pltpu.SemaphoreType.DMA((VARS * BLOCKS,)),
            pltpu.SemaphoreType.DMA((1,)),
        ],
        name="pack", limit=60
    )(live_rows, state)
    slabs = lax.all_to_all(chunks, "inst", 0, 0, tiled=True).reshape(INST, SENT, CELLS)
    ghosts = gathered_over_blocks(faces, ORDER)
    spatial, half_faces, mask = call(
        spatial_kernel,
        [(VARS, BLOCKS, ROWS, CELLS), (FACES * VARS, CELLS), (BLOCKS, ROWS, CELLS)],
        [SMEM, SMEM, SMEM, SMEM, VMEM, VMEM, VMEM, VMEM],
        [pltpu.VMEM((VARS, BLOCKS, ROWS, CELLS), jnp.float32)],
        name="spatial",
    )(live_rows, partner, row_jacobian, cell_jacobian, state, viscosity, local_step, ghosts)
    slabs, spatial = lax.optimization_barrier((slabs, spatial))
    (sent,) = call(
        slab_kernel, [(INST, MAIN, CELLS)], [HBM, HBM, HBM, VMEM, VMEM, VMEM],
        [
            pltpu.VMEM((INST, MAIN, CELLS), jnp.float32),
            pltpu.VMEM((INST, 96, CELLS), jnp.float32),
            LIVE,
            JACOBIAN,
            JACOBIAN,
            pltpu.SemaphoreType.DMA((3,)),
            pltpu.SemaphoreType.DMA((INST // GROUP,)),
        ],
        name="slab", out_specs=[HBM],
    )(live_rows, row_jacobian, cell_jacobian, slabs, viscosity, local_step)
    back = lax.all_to_all(sent, "inst", 0, 0, tiled=True)
    table = np.array([[spectral(t - s) for s in range(INST)] for t in range(INST)], np.float32)
    weights = jnp.asarray(np.repeat(table[:, :, None], CELLS, 2))
    (faces2,) = call(
        face_kernel, [(2 * FACES * VARS, CELLS)], [HBM, VMEM, VMEM, VMEM, VMEM],
        [LIVE, pltpu.SemaphoreType.DMA((1,))], name="faces"
    )(live_rows, weights, slabs, half_faces, local_step)
    ghosts2 = gathered_over_blocks(faces2, ORDER2)
    (spatial,) = call(
        ghost_kernel, [(VARS, BLOCKS, ROWS, CELLS)], [SMEM, SMEM, SMEM] + [VMEM] * 4, name="ghosts", aliases={6: 0}
    )(live_rows, partner, row_jacobian, viscosity, local_step, ghosts2, spatial)
    new_state, residual = call(
        final_kernel, [whole, whole], [VMEM] * 5,
        [pltpu.VMEM((VARS, BLOCKS, ROWS, CELLS), jnp.float32)] * 2 + [pltpu.SemaphoreType.DMA((4 * BLOCKS,))],
        name="final", out_specs=[HBM] * 2,
    )(state, local_step, mask, spatial, back)
    return new_state, residual


def solution(mesh):
    return jax.shard_map(
        per_device,
        mesh=mesh,
        in_specs=(
            P("inst", None, "blk", None, None),
            P(),
            P(),
            P("blk", None, None),
            P("blk", None, None),
            P(),
            P(),
        ),
        out_specs=(P("inst", None, "blk", None, None), P("inst", None, "blk", None, None)),
        check_vma=False,
    )
```
